128 devices in a mesh: outer: 16 (over z_hi, x, core), inner: 8 (over z_lo, y).
Axes of the slice: x: 4, y: 4, z: 4 (z_hi: 2, z_lo: 2; z = z_hi * 2 + z_lo), core: 2. Of those that a mesh axis runs over, the one named last changes fastest.
Arguments:
- tokens: bfloat16 [49152, 8192], P(('outer', 'inner')), may hold values from -6 to 6
- queries: bfloat16 [49152, 4096], P(('outer', 'inner')), may hold values from -6 to 6
- values: bfloat16 [49152, 512], P(('outer', 'inner')), may hold values from -6 to 6
- doc_ids: int32 [128, 384], P(('outer', 'inner')), may hold values from 0 to 3, never falling along the last dimension, each value on 1 to 192 neighbouring positions
- weight_codes: bfloat16 [8192, 512], P(('inner', 'outer')), may hold values from -15 to 15, as said below
- weight_scales: int32 [256, 512], P(('inner', 'outer')), may hold values from -11 to -8
- out_grad: bfloat16 [49152, 4096], P(('outer', 'inner')), may hold values from -6 to 6
Outputs:
- attn_out: bfloat16 [49152, 4096], P(('outer', 'inner'))
- grad_tokens: bfloat16 [49152, 8192], P(('outer', 'inner'))
- grad_weight: float32 [8192, 512], P(('inner', 'outer'))
The draws below stay inside these ranges and needn't reach their ends.
Inputs may be any that keep to these rules, and one draw needn't show every extreme that they name: `weight_codes`: each entry is plus or minus (1 + m / 8) * 2 ** e with whole m of 0 to 7 and e of -2 to 3.
All inputs are finite; a program needn't handle non-finite values.
Results may differ from the reference program's by a relative error of at most 0.023.
Values may be sent and summed in bfloat16 or wider, within the bound.
No kernel may reach another device: no remote copies, remote signals or barrier semaphores. Data moves between devices by JAX's collectives and lax.ppermute only.
A program may use at most 192 MiB of HBM per device.

```python
import math
import jax
import jax.numpy as jnp
import numpy as np
from jax import lax

D = 8192
KVH = 4
HD = 128
TOK_DEV = 384
GROUP = 8
KC = 512
QC = 4096
SEQS = 128
TOKENS = 49152


def draw_weight_codes(key, part):
    key = jax.random.fold_in(key, 11)
    key_mantissa, key_exponent, key_sign = jax.random.split(key, 3)
    mantissa = jax.random.randint(key_mantissa, (D, KC), 0, 8).astype(jnp.float32)
    exponent = jax.random.randint(key_exponent, (D, KC), -2, 4).astype(jnp.float32)
    signs_all = (jax.random.randint(key_sign, (D, KC), 0, 2) * 2 - 1).astype(jnp.float32)
    codes = signs_all * (1.0 + mantissa / 8.0) * jnp.exp2(exponent)
    return codes.astype(jnp.bfloat16)


def draw_tokens(key, part):
    key = jax.random.fold_in(key, 21)
    return jax.random.truncated_normal(key, -6.0, 6.0, (TOKENS, D), jnp.float32).astype(jnp.bfloat16)


def draw_queries(key, part):
    key = jax.random.fold_in(key, 23)
    return jax.random.truncated_normal(key, -6.0, 6.0, (TOKENS, QC), jnp.float32).astype(jnp.bfloat16)


def touch_ends(entries, key, low, largest):
    place = [jax.random.randint(jax.random.fold_in(key, axis), (), 0, length) for axis, length in enumerate(entries.shape)]
    longest = entries.shape.index(max(entries.shape))
    next_to = place[:longest] + [(place[longest] + 1) % entries.shape[longest]] + place[longest + 1:]
    return entries.at[tuple(place)].set(low).at[tuple(next_to)].set(largest)


def shard_levels(rng, extent, cuts, smallest, high):
    loudness = 1.0
    for position, shards_of in cuts:
        draws = jax.random.uniform(jax.random.fold_in(jax.random.fold_in(rng, 6), position), (shards_of,), jnp.float32, smallest / len(cuts), high / len(cuts))
        loudness = loudness * jnp.repeat(jnp.exp(draws), extent[position] // shards_of).reshape((-1,) + (1,) * (len(extent) - 1 - position))
    return loudness


def length_profile(count, total, limit, lean):
    loads = [(1 << 20) // math.isqrt(standing ** lean) + 1 for standing in range(2, count + 1)]
    surplus, counts = total - limit - (count - 1), [1] * (count - 1)
    while surplus > 0:
        free = [i for i in range(count - 1) if counts[i] < limit]
        whole, remaining = sum([loads[i] for i in free]), surplus
        for i in free:
            extra = min(limit - counts[i], max(1, remaining * loads[i] // whole), surplus)
            counts[i] = counts[i] + extra
            surplus = surplus - extra
    return np.array([limit] + counts)


def uneven(key, amount, total, most, skew):
    if amount == 2:
        one = jax.random.randint(key, (), max(1, total - most), min(most, total - 1) + 1)
        return jnp.stack([one, total - one])
    tallies = jnp.asarray(length_profile(amount, total, most, skew), jnp.int32)
    twos = (amount - 1) // 2
    source_of, taker = tallies[1:1 + 2 * twos:2], tallies[2:2 + 2 * twos:2]
    margin = jnp.minimum(source_of - 1, most - taker)
    moved = jax.random.randint(jax.random.fold_in(key, 1), (twos,), 0, 1 << 20) % (margin + 1)
    tallies = tallies.at[1:1 + 2 * twos:2].set(source_of - moved).at[2:2 + 2 * twos:2].set(taker + moved)
    return tallies[jax.random.permutation(jax.random.fold_in(key, 2), amount)]


def bell_draw(stream_key, extent, width, reach, pieces=(), kind=jnp.bfloat16):
    level = shard_levels(stream_key, extent, pieces, -0.22, 0.18) if pieces else 1.0
    drawn = jax.random.normal(stream_key, extent, jnp.float32) * width * level
    return jnp.minimum(jnp.maximum(drawn, -reach), reach).astype(kind)


def setup_inputs(seed: int = 0) -> dict:
    arg_keys = jax.random.split(jax.random.key(seed), 8)
    tokens = draw_tokens(jax.random.fold_in(arg_keys[7], 71), 0)
    queries = draw_queries(jax.random.fold_in(arg_keys[7], 71), 0)
    values = bell_draw(arg_keys[2], (TOKENS, KC), 1.0, 6.0, ((0, 128),))
    doc_ids = jax.vmap(lambda own: jnp.searchsorted(jnp.cumsum(uneven(own, 4, TOK_DEV, TOK_DEV // 2, 1)), jnp.arange(TOK_DEV), side="right"))(jax.random.split(arg_keys[3], SEQS)).reshape((SEQS, TOK_DEV)).astype(jnp.int32)
    weight_codes = draw_weight_codes(jax.random.fold_in(arg_keys[7], 71), 0)
    weight_scales = touch_ends(jax.random.randint(arg_keys[5], (D // 32, KC), -11, -7), jax.random.fold_in(arg_keys[5], 1), -11, (-7) - 1).astype(jnp.int32)
    out_grad = bell_draw(arg_keys[6], (TOKENS, QC), 1.0, 6.0, ((0, 128),))
    return dict(tokens=tokens, queries=queries, values=values, doc_ids=doc_ids, weight_codes=weight_codes, weight_scales=weight_scales, out_grad=out_grad)


def dequantize(codes, scales):
    factor = jnp.exp2(scales.astype(jnp.float32))
    rows = codes.shape[0]
    expanded = codes.astype(jnp.float32).reshape(rows // 32, 32, codes.shape[1]) * factor[:, None, :]
    return expanded.reshape(rows, codes.shape[1]).astype(jnp.bfloat16)

def attend(query_rows, key_rows, value_rows, grad_rows, doc_row):
    scale = HD ** (-0.5)
    query_heads = query_rows.astype(jnp.float32).reshape(TOK_DEV, KVH, GROUP, HD)
    key_heads = key_rows.astype(jnp.float32).reshape(TOK_DEV, KVH, HD)
    value_heads = value_rows.astype(jnp.float32).reshape(TOK_DEV, KVH, HD)
    grad_heads = grad_rows.astype(jnp.float32).reshape(TOK_DEV, KVH, GROUP, HD)
    positions = jnp.arange(TOK_DEV)
    allowed = (doc_row[:, None] == doc_row[None, :]) & (positions[:, None] >= positions[None, :])
    scores = jnp.einsum('tkgd,skd->kgts', query_heads, key_heads) * scale
    scores = jnp.where(allowed, scores, -1e+30)
    row_max = lax.optimization_barrier(jnp.max(scores, axis=-1, keepdims=True))
    unnormed = jnp.exp(scores - row_max)
    attn_probs = unnormed / lax.optimization_barrier(jnp.sum(unnormed, axis=-1, keepdims=True))
    probs_low = attn_probs.astype(jnp.bfloat16).astype(jnp.float32)
    output = jnp.einsum('kgts,skd->tkgd', probs_low, value_heads)
    output = output.reshape(TOK_DEV, QC).astype(jnp.bfloat16)
    dprobs = jnp.einsum('tkgd,skd->kgts', grad_heads, value_heads)
    delta = lax.optimization_barrier(jnp.sum(attn_probs * dprobs, axis=-1, keepdims=True))
    score_grad = (attn_probs * (dprobs - delta)).astype(jnp.bfloat16).astype(jnp.float32)
    key_grad = jnp.einsum('kgts,tkgd->skd', score_grad, query_heads) * scale
    return (output, key_grad.reshape(TOK_DEV, KC).astype(jnp.bfloat16))

def reference(tokens, queries, values, doc_ids, weight_codes, weight_scales, out_grad):
    tokens_full = tokens.astype(jnp.float32)
    inverse_rms = lax.rsqrt(lax.optimization_barrier(jnp.mean(tokens_full * tokens_full, axis=-1, keepdims=True)) + 1e-05)
    hat = tokens_full * inverse_rms
    normed = hat.astype(jnp.bfloat16)
    weight = dequantize(weight_codes, weight_scales)
    keys = jnp.dot(normed, weight, preferred_element_type=jnp.float32).astype(jnp.bfloat16)
    packed = (queries.reshape(SEQS, TOK_DEV, QC), keys.reshape(SEQS, TOK_DEV, KC), values.reshape(SEQS, TOK_DEV, KC), out_grad.reshape(SEQS, TOK_DEV, QC), doc_ids)
    outputs, key_grads = lax.map(lambda item: attend(*item), packed)
    attn_out = outputs.reshape(TOKENS, QC)
    dkeys = key_grads.reshape(TOKENS, KC)
    grad_weight = lax.dot_general(normed, dkeys, (((0,), (0,)), ((), ())), preferred_element_type=jnp.float32)
    dnormed = lax.dot_general(dkeys, weight, (((1,), (1,)), ((), ())), preferred_element_type=jnp.float32)
    grad_tokens = (inverse_rms * (dnormed - hat * lax.optimization_barrier(jnp.mean(dnormed * hat, axis=-1, keepdims=True)))).astype(jnp.bfloat16)
    return (attn_out, grad_tokens, grad_weight)
```

```python
import math

import jax
import jax.numpy as jnp
import numpy as np
from jax import lax
from jax.experimental import pallas as pl
from jax.experimental.pallas import tpu as pltpu
from jax.sharding import PartitionSpec as P

HD = 128
GROUP = 8
BLK = 512
AXES = ("outer", "inner")
F32 = jnp.float32
BF16 = jnp.bfloat16
VMEM_LIMIT = 48 * 1024 * 1024

INDEX = np.arange(128).reshape(2, 4, 2, 2, 4)


def permutation(move):
    pairs = []
    for zh in range(2):
        for x in range(4):
            for c in range(2):
                for zl in range(2):
                    for y in range(4):
                        nx, ny, nz, nc = move(x, y, zh * 2 + zl, c)
                        nx, ny, nz = nx % 4, ny % 4, nz % 4
                        target = INDEX[nz // 2, nx, nc, nz % 2, ny]
                        pairs.append((int(INDEX[zh, x, c, zl, y]), int(target)))
    return pairs


SWAP = permutation(lambda x, y, z, c: (x, y, z, 1 - c))


def along_x(d):
    return permutation(lambda x, y, z, c: (x + d, y, z, c))


def along_u(d):
    return permutation(lambda x, y, z, c: (x, y + d * (1 - c), z + d * c, c))


def along_v(d):
    return permutation(lambda x, y, z, c: (x, y + d * c, z + d * (1 - c), c))


def permute(a, perm):
    return lax.ppermute(a, AXES, perm)


def collect(a, along):
    return [a, permute(a, along(-1)), permute(a, along(2)), permute(a, along(1))]


def distribute(parts, along):
    return [permute(parts[2], along(2)), permute(parts[1], along(1)), permute(parts[3], along(-1))]


def params(**kw):
    return pltpu.CompilerParams(vmem_limit_bytes=VMEM_LIMIT, **kw)


def keys_part(order, own, sib, w, acc, rv):
    rows = own.shape[0]
    cols = w.shape[-1]
    first = acc is None

    def kernel(order_ref, own_ref, sib_ref, w_ref, *rest):
        out_own, out_sib = rest[-2:]
        i = pl.program_id(0)
        a = jnp.dot(own_ref[...], w_ref[0], preferred_element_type=F32)
        b = jnp.dot(sib_ref[...], w_ref[0], preferred_element_type=F32)

        @pl.when(i == 0)
        def _():
            if first:
                out_own[...] = a
                out_sib[...] = b
            else:
                out_own[...] = rest[0][...] + a
                out_sib[...] = rest[1][...] + b

        @pl.when(i > 0)
        def _():
            out_own[...] += a
            out_sib[...] += b

    tok = pl.BlockSpec((rows, BLK), lambda i, o: (0, o[rv * 4 + i]))
    whole = pl.BlockSpec((rows, cols), lambda i, o: (0, 0))
    out = jax.ShapeDtypeStruct((rows, cols), F32)
    return pl.pallas_call(
        kernel,
        out_shape=(out, out),
        grid_spec=pltpu.PrefetchScalarGridSpec(
            num_scalar_prefetch=1,
            grid=(4,),
            in_specs=[tok, tok, pl.BlockSpec((1, BLK, cols), lambda i, o: (i, 0, 0))]
            + ([] if first else [whole, whole]),
            out_specs=(whole, whole),
        ),
        compiler_params=params(),
        cost_estimate=pl.CostEstimate(
            flops=4 * rows * cols * BLK * 4, bytes_accessed=rows * BLK * 16, transcendentals=0
        ),
        name="keys_part",
    )(order, own, sib, w, *(() if first else acc))


def attention(kv, queries, keys_raw, values, out_grad, inv, doc_row, doc_col, prev):
    rows = queries.shape[0]
    scale = HD ** (-0.5)
    first = prev is None
    pairs = GROUP // 2

    def kernel(kv_ref, q_ref, k_ref, v_ref, g_ref, inv_ref, row_ref, col_ref, *rest):
        if not first:
            rest = rest[1:]
        o_ref, dkb_ref, dkw_ref, ms_ref, acc, bias, kb, vt, msum = rest
        h, i = pl.program_id(0), pl.program_id(1)

        @pl.when((h == 0) & (i == 0))
        def _():
            s = lax.broadcasted_iota(jnp.int32, (rows, rows), 0)
            t = lax.broadcasted_iota(jnp.int32, (rows, rows), 1)
            ok = (s <= t) & (col_ref[...] == row_ref[...])
            bias[...] = jnp.where(ok, 0.0, -1e30).astype(F32)
            msum[...] = jnp.zeros_like(msum)

        @pl.when(i == 0)
        def _():
            kb[...] = (k_ref[...] * inv_ref[...] * (scale * math.log2(math.e))).astype(BF16)
            vt[...] = v_ref[...].astype(F32).T.astype(BF16)
            acc[...] = jnp.zeros_like(acc)

        for j in range(rows // HD):
            n = (j + 1) * HD
            ts = slice(j * HD, n)
            q = jnp.concatenate([q_ref[ts, :HD], q_ref[ts, HD:]], axis=0)
            g = jnp.concatenate([g_ref[ts, :HD], g_ref[ts, HD:]], axis=0)
            sc = lax.dot_general(kb[:n], q, (((1,), (1,)), ((), ())), preferred_element_type=F32)
            b = bias[:n, ts]
            sc = sc + jnp.concatenate([b, b], axis=1)
            top = jnp.max(sc, axis=0, keepdims=True)
            e = jnp.exp2(sc - top)
            p = e * (1.0 / jnp.sum(e, axis=0, keepdims=True))
            ot = jnp.dot(vt[:, :n], p.astype(BF16), preferred_element_type=F32)
            o = ot.T.astype(BF16)
            o_ref[ts, :HD] = o[:HD]
            o_ref[ts, HD:] = o[HD:]
            dp = lax.dot_general(
                v_ref[:n], g, (((1,), (1,)), ((), ())), preferred_element_type=F32
            )
            pd = p * dp
            ds = (pd - p * jnp.sum(pd, axis=0, keepdims=True)).astype(BF16)
            acc[:n] += jnp.dot(ds, q, preferred_element_type=F32)

        @pl.when(i == pairs - 1)
        def _():
            dk = acc[...] * scale
            dkb = dk.astype(BF16)
            dkb_ref[...] = dkb
            dkw_ref[...] = (dk * inv_ref[...]).astype(BF16)
            msum[...] += jnp.sum(
                dkb.astype(F32) * (k_ref[...] * inv_ref[...]), axis=1, keepdims=True
            )
            ms_ref[...] = msum[...]

    wide = pl.BlockSpec((rows, 2 * HD), lambda h, i, kv: (0, (kv[0] + h) * pairs + i))
    half = pl.BlockSpec((rows, HD), lambda h, i, kv: (0, h))
    one = pl.BlockSpec((rows, 1), lambda h, i, kv: (0, 0))
    cols = 2 * HD
    return pl.pallas_call(
        kernel,
        out_shape=(
            jax.ShapeDtypeStruct(queries.shape, BF16),
            jax.ShapeDtypeStruct((rows, cols), BF16),
            jax.ShapeDtypeStruct((rows, cols), BF16),
            jax.ShapeDtypeStruct((rows, 1), F32),
        ),
        grid_spec=pltpu.PrefetchScalarGridSpec(
            num_scalar_prefetch=1,
            grid=(2, pairs),
            in_specs=[
                wide,
                half,
                pl.BlockSpec((rows, HD), lambda h, i, kv: (0, kv[0] + h)),
                wide,
                one,
                pl.BlockSpec((1, rows), lambda h, i, kv: (0, 0)),
                one,
            ]
            + ([] if first else [pl.BlockSpec(memory_space=pl.ANY)]),
            out_specs=(wide, half, half, one),
            scratch_shapes=[
                pltpu.VMEM((rows, HD), F32),
                pltpu.VMEM((rows, rows), F32),
                pltpu.VMEM((rows, HD), BF16),
                pltpu.VMEM((HD, rows), BF16),
                pltpu.VMEM((rows, 1), F32),
            ],
        ),
        input_output_aliases={} if first else {8: 0},
        compiler_params=params(),
        cost_estimate=pl.CostEstimate(
            flops=8 * 16 * rows * rows * HD * 2 // 3,
            bytes_accessed=rows * 2048 * 6,
            transcendentals=16 * rows * rows * 2 // 3,
        ),
        name="attention",
    )(kv, queries, keys_raw, values, out_grad, inv, doc_row, doc_col, *(() if first else (prev,)))


def grad_part(order, own, sib, dk_own, dk_sib, rv):
    rows = own.shape[0]
    cols = dk_own.shape[1]

    def kernel(order_ref, own_ref, sib_ref, a_ref, b_ref, out, at, bt):
        @pl.when(pl.program_id(0) == 0)
        def _():
            at[...] = a_ref[...].astype(F32).T.astype(BF16)
            bt[...] = b_ref[...].astype(F32).T.astype(BF16)

        out[0] = (
            jnp.dot(at[...], own_ref[...], preferred_element_type=F32)
            + jnp.dot(bt[...], sib_ref[...], preferred_element_type=F32)
        ).astype(BF16)

    tok = pl.BlockSpec((rows, BLK), lambda i, o: (0, o[rv * 4 + i]))
    whole = pl.BlockSpec((rows, cols), lambda i, o: (0, 0))
    return pl.pallas_call(
        kernel,
        out_shape=jax.ShapeDtypeStruct((4, cols, BLK), BF16),
        grid_spec=pltpu.PrefetchScalarGridSpec(
            num_scalar_prefetch=1,
            grid=(4,),
            in_specs=[tok, tok, whole, whole],
            out_specs=pl.BlockSpec((1, cols, BLK), lambda i, o: (i, 0, 0)),
            scratch_shapes=[pltpu.VMEM((cols, rows), BF16), pltpu.VMEM((cols, rows), BF16)],
        ),
        compiler_params=params(),
        cost_estimate=pl.CostEstimate(
            flops=4 * rows * cols * BLK * 4, bytes_accessed=rows * BLK * 16, transcendentals=0
        ),
        name="grad_part",
    )(order, own, sib, dk_own, dk_sib)


def token_grad(order, tokens, dk_own, dk_oth, w_own, w_sib, inv, ms0, ms1):
    rows, width = tokens.shape
    cols = dk_own.shape[1]

    def kernel(order_ref, tok_ref, a_ref, b_ref, *rest):
        own, sib = rest[:4], rest[4:8]
        inv_ref, ms0_ref, ms1_ref, out, wo, ws = rest[8:]
        i = pl.program_id(0)
        for k in range(4):

            @pl.when(i // 4 == k)
            def _(k=k):
                wo[...] = own[k][0]

            @pl.when(i % 4 == k)
            def _(k=k):
                ws[...] = sib[k][0]

        nt = (((1,), (1,)), ((), ()))
        dn = lax.dot_general(a_ref[...], wo[...], nt, preferred_element_type=F32)
        dn = dn + lax.dot_general(b_ref[...], ws[...], nt, preferred_element_type=F32)
        r = inv_ref[...]
        mean = (ms0_ref[...] + ms1_ref[...]) * (1.0 / width)
        hat = tok_ref[...].astype(F32) * r
        out[...] = (r * (dn - hat * mean)).astype(BF16)

    tok = pl.BlockSpec((rows, BLK), lambda i, o: (0, o[i]))
    whole = pl.BlockSpec((rows, cols), lambda i, o: (0, 0))
    one = pl.BlockSpec((rows, 1), lambda i, o: (0, 0))
    own_specs = [
        pl.BlockSpec((1, BLK, cols), lambda i, o, k=k: (jnp.clip(i - 4 * k, 0, 3), 0, 0))
        for k in range(4)
    ]
    sib_specs = [pl.BlockSpec((1, BLK, cols), lambda i, o: (i // 4, 0, 0)) for _ in range(4)]
    return pl.pallas_call(
        kernel,
        out_shape=jax.ShapeDtypeStruct(tokens.shape, BF16),
        grid_spec=pltpu.PrefetchScalarGridSpec(
            num_scalar_prefetch=1,
            grid=(16,),
            in_specs=[tok, whole, whole] + own_specs + sib_specs + [one, one, one],
            out_specs=tok,
            scratch_shapes=[pltpu.VMEM((BLK, cols), BF16), pltpu.VMEM((BLK, cols), BF16)],
        ),
        compiler_params=params(),
        cost_estimate=pl.CostEstimate(
            flops=4 * rows * cols * width, bytes_accessed=rows * width * 5, transcendentals=0
        ),
        name="token_grad",
    )(order, tokens, dk_own, dk_oth, *w_own, *w_sib, inv, ms0, ms1)


def per_device(tokens, queries, values, doc_ids, weight_codes, weight_scales, out_grad):
    rows, width = tokens.shape
    outer, inner = lax.axis_index("outer"), lax.axis_index("inner")
    x, core, y = (outer // 2) % 4, outer % 2, inner % 4
    z = (outer // 8) * 2 + inner // 4
    u, v = jnp.where(core == 0, y, z), jnp.where(core == 0, z, y)
    bv = (v + jnp.arange(4, dtype=jnp.int32)[:, None]) % 4
    bu = (u + jnp.arange(4, dtype=jnp.int32)[None, :]) % 4
    by, bz = jnp.where(core == 0, bu, bv), jnp.where(core == 0, bv, bu)
    order = (((bz % 2) * 4 + by) * 2 + bz // 2).reshape(16).astype(jnp.int32)

    factor = jnp.exp2(weight_scales.astype(F32))
    wrows, wcols = weight_codes.shape
    weight = weight_codes.astype(F32).reshape(2, wrows // 2, wcols) * factor[:, None, :]
    weight = weight.reshape(wrows, wcols).astype(BF16)
    hc = wcols // 2
    keep = jnp.where(core == 0, weight[:, :hc], weight[:, hc:])
    send = jnp.where(core == 0, weight[:, hc:], weight[:, :hc])
    got = permute(send, SWAP)
    chip = jnp.where(
        core == 0, jnp.concatenate([keep, got], 0), jnp.concatenate([got, keep], 0)
    )
    ring = collect(chip, along_x)
    ordered = []
    for i in range(4):
        r = (i - x) % 4
        ordered.append(
            jnp.where(r == 0, ring[0], jnp.where(r == 1, ring[1], jnp.where(r == 2, ring[2], ring[3])))
        )
    block = jnp.concatenate(ordered, 0)
    plane = jnp.stack(collect(block, along_u))
    w_own = collect(plane, along_v)

    tokens_sib = permute(tokens, SWAP)
    full = tokens.astype(F32)
    inv = lax.rsqrt(jnp.mean(full * full, axis=-1, keepdims=True) + 1e-05)

    acc = None
    for rv in (0, 1, 3, 2):
        acc = keys_part(order, tokens, tokens_sib, w_own[rv], acc, rv)
    keys_own, keys_sib = acc
    keys_oth = permute(keys_sib, SWAP)
    w_sib = [permute(w, SWAP) for w in w_own]

    doc_row = doc_ids
    doc_col = doc_ids.reshape(rows, 1)
    kv_own = (core * 2).astype(jnp.int32).reshape(1)
    kv_oth = 2 - kv_own
    out, dkb_own, dkw_own, ms_own = attention(
        kv_own, queries, keys_own, values, out_grad, inv, doc_row, doc_col, None
    )
    out, dkb_oth, dkw_oth, ms_oth = attention(
        kv_oth, queries, keys_oth, values, out_grad, inv, doc_row, doc_col, out
    )
    dkw_sib = permute(dkw_oth, SWAP)

    parts = [None] * 4
    for rv in (2, 1, 3, 0):
        parts[rv] = grad_part(order, tokens, tokens_sib, dkw_own, dkw_sib, rv)
    arrived = distribute(parts, along_v)
    grad_tokens = token_grad(
        order, tokens, dkb_own, dkb_oth, w_own, w_sib, inv, ms_own, ms_oth
    )

    def total(own, others):
        s = own.astype(F32)
        for o in others:
            s = s + o.astype(F32)
        return s

    chunk = [total(parts[0][r], [a[r] for a in arrived]) for r in range(4)]
    arrived = distribute([c.astype(BF16) for c in chunk], along_u)
    line = total(chunk[0], arrived)
    by_x = [lax.dynamic_slice_in_dim(line, ((x + r) % 4) * HD, HD, 1) for r in range(4)]
    arrived = distribute([c.astype(BF16) for c in by_x], along_x)
    mine = total(by_x[0], arrived).T
    keep = lax.dynamic_slice_in_dim(mine, core * wrows, wrows, 0)
    got = permute(lax.dynamic_slice_in_dim(mine, (1 - core) * wrows, wrows, 0), SWAP)
    grad_weight = jnp.where(
        core == 0, jnp.concatenate([keep, got], 1), jnp.concatenate([got, keep], 1)
    )
    return (out, grad_tokens, grad_weight)


def solution(mesh):
    return jax.shard_map(
        per_device,
        mesh=mesh,
        in_specs=(
            P(("outer", "inner"), None),
            P(("outer", "inner"), None),
            P(("outer", "inner"), None),
            P(("outer", "inner"), None),
            P(("inner", "outer"), None),
            P(("inner", "outer"), None),
            P(("outer", "inner"), None),
        ),
        out_specs=(
            P(("outer", "inner"), None),
            P(("outer", "inner"), None),
            P(("inner", "outer"), None),
        ),
        check_vma=False,
    )
```

```python
import math

import jax
import jax.numpy as jnp
import numpy as np
from jax import lax
from jax.experimental import pallas as pl
from jax.experimental.pallas import tpu as pltpu
from jax.sharding import PartitionSpec as P

HD = 128
GROUP = 8
BLK = 512
AXES = ("outer", "inner")
F32 = jnp.float32
BF16 = jnp.bfloat16
VMEM_LIMIT = 48 * 1024 * 1024
ATTENTION_LIMIT = 56 * 1024 * 1024

INDEX = np.arange(128).reshape(2, 4, 2, 2, 4)


def permutation(move):
    pairs = []
    for zh in range(2):
        for x in range(4):
            for c in range(2):
                for zl in range(2):
                    for y in range(4):
                        nx, ny, nz, nc = move(x, y, zh * 2 + zl, c)
                        nx, ny, nz = nx % 4, ny % 4, nz % 4
                        target = INDEX[nz // 2, nx, nc, nz % 2, ny]
                        pairs.append((int(INDEX[zh, x, c, zl, y]), int(target)))
    return pairs


SWAP = permutation(lambda x, y, z, c: (x, y, z, 1 - c))


def along_x(d):
    return permutation(lambda x, y, z, c: (x + d, y, z, c))


def along_u(d):
    return permutation(lambda x, y, z, c: (x, y + d * (1 - c), z + d * c, c))


def along_v(d):
    return permutation(lambda x, y, z, c: (x, y + d * c, z + d * (1 - c), c))


def permute(a, perm):
    return lax.ppermute(a, AXES, perm)


def collect(a, along):
    return [a, permute(a, along(-1)), permute(a, along(2)), permute(a, along(1))]


def distribute(parts, along):
    return [permute(parts[2], along(2)), permute(parts[1], along(1)), permute(parts[3], along(-1))]


def params(**kw):
    return pltpu.CompilerParams(vmem_limit_bytes=VMEM_LIMIT, **kw)


def prepare(tokens, doc_ids):
    rows, width = tokens.shape
    steps = 4

    def kernel(tok_ref, doc_ref, inv_ref, bias_ref):
        i = pl.program_id(0)
        a = tok_ref[...].astype(F32)
        part = jnp.sum(a * a, axis=1, keepdims=True)

        @pl.when(i == 0)
        def _():
            row = jnp.broadcast_to(doc_ref[...].astype(F32), (rows, rows))
            s = lax.broadcasted_iota(jnp.int32, (rows, rows), 0)
            t = lax.broadcasted_iota(jnp.int32, (rows, rows), 1)
            bias_ref[...] = jnp.where((s <= t) & (row == row.T), 0.0, -1e30).astype(F32)
            inv_ref[...] = part

        @pl.when(i > 0)
        def _():
            inv_ref[...] += part

        @pl.when(i == steps - 1)
        def _():
            inv_ref[...] = lax.rsqrt(inv_ref[...] * (1.0 / width) + 1e-05)

    return pl.pallas_call(
        kernel,
        out_shape=(
            jax.ShapeDtypeStruct((rows, 1), F32),
            jax.ShapeDtypeStruct((rows, rows), F32),
        ),
        grid=(steps,),
        in_specs=[
            pl.BlockSpec((rows, width // steps), lambda i: (0, i)),
            pl.BlockSpec((1, rows), lambda i: (0, 0)),
        ],
        out_specs=(
            pl.BlockSpec((rows, 1), lambda i: (0, 0)),
            pl.BlockSpec((rows, rows), lambda i: (0, 0)),
        ),
        compiler_params=params(),
        cost_estimate=pl.CostEstimate(
            flops=rows * width * 3, bytes_accessed=rows * width * 2, transcendentals=0
        ),
        name="prepare",
    )(tokens, doc_ids)


def keys_part(order, own, sib, ws, acc, base):
    rows = own.shape[0]
    cols = ws[0].shape[-1]
    first = acc is None
    n = len(ws)

    def kernel(order_ref, *refs):
        tok_refs, w_refs = refs[:8], refs[8 : 8 + n]
        rest = refs[8 + n :]
        out_own, out_sib = rest[-2:]
        i = pl.program_id(0)
        x = jnp.concatenate(
            [jnp.concatenate([tok_refs[4 * s + k][...] for k in range(4)], 1) for s in range(2)], 0
        )

        def add(w, start):
            p = jnp.dot(x, w.reshape(4 * BLK, cols), preferred_element_type=F32)
            if start and first:
                out_own[...] = p[:rows]
                out_sib[...] = p[rows:]
            elif start:
                out_own[...] = rest[0][...] + p[:rows]
                out_sib[...] = rest[1][...] + p[rows:]
            else:
                out_own[...] += p[:rows]
                out_sib[...] += p[rows:]

        for k in range(n):

            @pl.when(i == k)
            def _(k=k):
                add(w_refs[k][...], k == 0)

    tok = [
        pl.BlockSpec((rows, BLK), lambda i, o, k=k: (0, o[(base + i) * 4 + k])) for k in range(4)
    ]
    whole = pl.BlockSpec((rows, cols), lambda i, o: (0, 0))
    wspec = pl.BlockSpec((4, BLK, cols), lambda i, o: (0, 0, 0))
    out = jax.ShapeDtypeStruct((rows, cols), F32)
    return pl.pallas_call(
        kernel,
        out_shape=(out, out),
        grid_spec=pltpu.PrefetchScalarGridSpec(
            num_scalar_prefetch=1,
            grid=(n,),
            in_specs=tok + tok + [wspec] * n + ([] if first else [whole, whole]),
            out_specs=(whole, whole),
        ),
        compiler_params=params(),
        cost_estimate=pl.CostEstimate(
            flops=4 * n * rows * cols * BLK * 4,
            bytes_accessed=n * rows * BLK * 16,
            transcendentals=0,
        ),
        name="keys_part",
    )(order, *[own] * 4, *[sib] * 4, *ws, *(() if first else acc))


def attention(queries, keys_own, keys_oth, values, out_grad, inv, bias):
    rows = queries.shape[0]
    scale = HD ** (-0.5)
    cols = keys_own.shape[1]

    def kernel(q_ref, ko_ref, kt_ref, v_ref, g_ref, inv_ref, bias, *rest):
        o_ref, dk_ref, dwo_ref, dwt_ref, ms_ref, acc, kf = rest
        h = pl.program_id(0)
        core = lax.axis_index("outer") % 2
        is_own = h // 2 == core
        at = pl.ds(pl.multiple_of((h % 2) * HD, HD), HD)

        @pl.when(h == 0)
        def _():
            ms_ref[...] = jnp.zeros_like(ms_ref)

        @pl.when(is_own)
        def _():
            kf[...] = ko_ref[:, at] * inv_ref[...]

        @pl.when(jnp.logical_not(is_own))
        def _():
            kf[...] = kt_ref[:, at] * inv_ref[...]

        kb = (kf[...] * (scale * math.log2(math.e))).astype(BF16)
        vb = v_ref[...]
        vt = vb.astype(F32).T.astype(BF16)
        acc[...] = jnp.zeros_like(acc)
        for j in range(rows // HD):
            n = (j + 1) * HD
            ts = slice(j * HD, n)
            cut = [slice(a * HD, (a + 1) * HD) for a in range(GROUP)]
            q = jnp.concatenate([q_ref[ts, c] for c in cut], axis=0)
            g = jnp.concatenate([g_ref[ts, c] for c in cut], axis=0)
            sc = lax.dot_general(kb[:n], q, (((1,), (1,)), ((), ())), preferred_element_type=F32)
            sc = sc + jnp.concatenate([bias[:n, ts]] * GROUP, axis=1)
            top = jnp.max(sc, axis=0, keepdims=True)
            e = jnp.exp2(sc - top)
            p = e * (1.0 / jnp.sum(e, axis=0, keepdims=True))
            ot = jnp.dot(vt[:, :n], p.astype(BF16), preferred_element_type=F32)
            o = ot.T.astype(BF16)
            for c in cut:
                o_ref[ts, c] = o[c]
            dp = lax.dot_general(vb[:n], g, (((1,), (1,)), ((), ())), preferred_element_type=F32)
            pd = p * dp
            ds = (pd - p * jnp.sum(pd, axis=0, keepdims=True)).astype(BF16)
            acc[:n] += jnp.dot(ds, q, preferred_element_type=F32)
        dk = acc[...] * scale
        dkb = dk.astype(BF16)
        dkw = (dk * inv_ref[...]).T.astype(BF16)
        ms_ref[...] += jnp.sum(dkb.astype(F32) * kf[...], axis=1, keepdims=True)

        @pl.when(is_own)
        def _():
            dk_ref[:, at] = dkb
            dwo_ref[at, :] = dkw

        @pl.when(jnp.logical_not(is_own))
        def _():
            dk_ref[:, pl.ds(pl.multiple_of((h % 2) * HD + cols, HD), HD)] = dkb
            dwt_ref[at, :] = dkw

    wide = pl.BlockSpec((rows, GROUP * HD), lambda h: (0, h))
    head = pl.BlockSpec((rows, HD), lambda h: (0, h))

    def whole(*shape):
        return pl.BlockSpec(shape, lambda h: (0, 0))

    half = whole(rows, cols)
    halft = whole(cols, rows)
    one = whole(rows, 1)
    return pl.pallas_call(
        kernel,
        out_shape=(
            jax.ShapeDtypeStruct(queries.shape, BF16),
            jax.ShapeDtypeStruct((rows, 2 * cols), BF16),
            jax.ShapeDtypeStruct((cols, rows), BF16),
            jax.ShapeDtypeStruct((cols, rows), BF16),
            jax.ShapeDtypeStruct((rows, 1), F32),
        ),
        grid=(4,),
        in_specs=[wide, half, half, head, wide, one, whole(rows, rows)],
        out_specs=(wide, whole(rows, 2 * cols), halft, halft, one),
        scratch_shapes=[pltpu.VMEM((rows, HD), F32), pltpu.VMEM((rows, HD), F32)],
        compiler_params=pltpu.CompilerParams(vmem_limit_bytes=ATTENTION_LIMIT),
        cost_estimate=pl.CostEstimate(
            flops=8 * 32 * rows * rows * HD * 2 // 3,
            bytes_accessed=rows * 4096 * 6,
            transcendentals=32 * rows * rows * 2 // 3,
        ),
        name="attention",
    )(queries, keys_own, keys_oth, values, out_grad, inv, bias)


def grad_part(order, own, sib, dk_own, dk_sib, rvs):
    cols, rows = dk_own.shape
    n = len(rvs)

    def kernel(order_ref, *refs):
        own_refs, sib_refs = refs[:4], refs[4:8]
        a_ref, b_ref, *outs = refs[8:]
        dk = jnp.concatenate([a_ref[...], b_ref[...]], 1)
        i = pl.program_id(0)
        for k in range(4):
            x = jnp.concatenate([own_refs[k][...], sib_refs[k][...]], 0)
            p = jnp.dot(dk, x, preferred_element_type=F32).astype(BF16)
            for m in range(n):

                @pl.when(i == m)
                def _(m=m):
                    outs[m][k] = p

    base = rvs[0]
    by = rvs[1] - rvs[0] if n > 1 else 0
    tok = [
        pl.BlockSpec((rows, BLK), lambda i, o, k=k: (0, o[(base + by * i) * 4 + k]))
        for k in range(4)
    ]
    half = pl.BlockSpec((cols, rows), lambda i, o: (0, 0))
    return pl.pallas_call(
        kernel,
        out_shape=tuple(jax.ShapeDtypeStruct((4, cols, BLK), BF16) for _ in rvs),
        grid_spec=pltpu.PrefetchScalarGridSpec(
            num_scalar_prefetch=1,
            grid=(n,),
            in_specs=tok + tok + [half, half],
            out_specs=tuple(pl.BlockSpec((4, cols, BLK), lambda i, o: (0, 0, 0)) for _ in rvs),
        ),
        compiler_params=params(),
        cost_estimate=pl.CostEstimate(
            flops=4 * n * rows * cols * BLK * 4,
            bytes_accessed=n * rows * BLK * 16,
            transcendentals=0,
        ),
        name="grad_part",
    )(order, *[own] * 4, *[sib] * 4, dk_own, dk_sib)


def token_grad(place, tokens, dk, w_own, w_sib, inv, ms):
    rows, width = tokens.shape
    cols = w_own[0].shape[-1]
    step = 2

    def kernel(place_ref, tok_ref, dk_ref, *rest):
        own, sib = rest[:4], rest[4:8]
        inv_ref, ms_ref, out, w = rest[8:]
        i = pl.program_id(0)

        @pl.when(i == 0)
        def _():
            for k in range(4):
                w[4 * k : 4 * k + 4, :, :cols] = own[k][...]
            for k in range(4):
                for m in range(4):
                    w[4 * m + k, :, cols:] = sib[k][m]

        r = inv_ref[...]
        mean = ms_ref[...] * (r * r * (1.0 / width))
        for k in range(step):
            dn = lax.dot_general(
                dk_ref[...],
                w[place_ref[i * step + k]],
                (((1,), (1,)), ((), ())),
                preferred_element_type=F32,
            )
            c = slice(k * BLK, (k + 1) * BLK)
            out[:, c] = (r * dn - tok_ref[:, c].astype(F32) * mean).astype(BF16)

    tok = pl.BlockSpec((rows, BLK * step), lambda i, o: (0, i))
    one = pl.BlockSpec((rows, 1), lambda i, o: (0, 0))
    wspec = pl.BlockSpec((4, BLK, cols), lambda i, o: (0, 0, 0))
    return pl.pallas_call(
        kernel,
        out_shape=jax.ShapeDtypeStruct(tokens.shape, BF16),
        grid_spec=pltpu.PrefetchScalarGridSpec(
            num_scalar_prefetch=1,
            grid=(16 // step,),
            in_specs=[tok, pl.BlockSpec((rows, 2 * cols), lambda i, o: (0, 0))]
            + [wspec] * 8
            + [one, one],
            out_specs=tok,
            scratch_shapes=[pltpu.VMEM((16, BLK, 2 * cols), BF16)],
        ),
        compiler_params=params(),
        cost_estimate=pl.CostEstimate(
            flops=4 * rows * cols * width, bytes_accessed=rows * width * 5, transcendentals=0
        ),
        name="token_grad",
    )(place, tokens, dk, *w_own, *w_sib, inv, ms)


def per_device(tokens, queries, values, doc_ids, weight_codes, weight_scales, out_grad):
    rows, width = tokens.shape
    outer, inner = lax.axis_index("outer"), lax.axis_index("inner")
    x, core, y = (outer // 2) % 4, outer % 2, inner % 4
    z = (outer // 8) * 2 + inner // 4
    u, v = jnp.where(core == 0, y, z), jnp.where(core == 0, z, y)
    ring4 = jnp.arange(4, dtype=jnp.int32)
    bv, bu = (v + ring4[:, None]) % 4, (u + ring4[None, :]) % 4
    by, bz = jnp.where(core == 0, bu, bv), jnp.where(core == 0, bv, bu)
    order = (((bz % 2) * 4 + by) * 2 + bz // 2).reshape(16).astype(jnp.int32)
    q = jnp.arange(16, dtype=jnp.int32)
    ry, rz = (q // 2 - y) % 4, ((q % 2) * 2 + q // 8 - z) % 4
    rv, ru = jnp.where(core == 0, rz, ry), jnp.where(core == 0, ry, rz)
    place = (rv * 4 + ru).astype(jnp.int32)

    factor = jnp.exp2(weight_scales.astype(F32))
    wrows, wcols = weight_codes.shape
    weight = weight_codes.astype(F32).reshape(2, wrows // 2, wcols) * factor[:, None, :]
    weight = weight.reshape(wrows, wcols).astype(BF16)
    hc = wcols // 2
    keep = jnp.where(core == 0, weight[:, :hc], weight[:, hc:])
    send = jnp.where(core == 0, weight[:, hc:], weight[:, :hc])
    got = permute(send, SWAP)
    chip = jnp.where(
        core == 0, jnp.concatenate([keep, got], 0), jnp.concatenate([got, keep], 0)
    )
    ring = collect(chip, along_x)
    ordered = []
    for i in range(4):
        r = (i - x) % 4
        ordered.append(
            jnp.where(r == 0, ring[0], jnp.where(r == 1, ring[1], jnp.where(r == 2, ring[2], ring[3])))
        )
    block = jnp.concatenate(ordered, 0)
    tokens_later, block = lax.optimization_barrier((tokens, block))
    tokens_sib = permute(tokens_later, SWAP)
    inv, bias = prepare(tokens, doc_ids)
    plane = jnp.stack(collect(block, along_u))
    plane, inv, bias, tokens_sib, order, place = lax.optimization_barrier(
        (plane, inv, bias, tokens_sib, order, place)
    )
    w_own = collect(plane, along_v)

    acc = keys_part(order, tokens, tokens_sib, w_own[:1], None, 0)
    w_own[1], w_own[2], w_own[3], *acc = lax.optimization_barrier(
        (w_own[1], w_own[2], w_own[3], *acc)
    )
    keys_own, keys_sib = keys_part(order, tokens, tokens_sib, w_own[1:], acc, 1)
    keys_oth = permute(keys_sib, SWAP)
    w_sib = [permute(w, SWAP) for w in w_own]

    out, dk, dkw_own, dkw_oth, ms = attention(
        queries, keys_own, keys_oth, values, out_grad, inv, bias
    )
    dkw_oth, *w_sib = lax.optimization_barrier((dkw_oth, *w_sib))
    dkw_sib = permute(dkw_oth, SWAP)

    parts = [None] * 4
    for rvs in ((2,), (1, 3), (0,)):
        for r, part in zip(rvs, grad_part(order, tokens, tokens_sib, dkw_own, dkw_sib, rvs)):
            parts[r] = part
    arrived = distribute(parts, along_v)
    grad_tokens = token_grad(place, tokens, dk, w_own, w_sib, inv, ms)
    grad_tokens, parts[0], *arrived = lax.optimization_barrier((grad_tokens, parts[0], *arrived))

    def total(own, others):
        s = own.astype(F32)
        for o in others:
            s = s + o.astype(F32)
        return s

    chunk = [total(parts[0][r], [a[r] for a in arrived]) for r in range(4)]
    arrived = distribute([c.astype(BF16) for c in chunk], along_u)
    line = total(chunk[0], arrived)
    by_x = [lax.dynamic_slice_in_dim(line, ((x + r) % 4) * HD, HD, 1) for r in range(4)]
    arrived = distribute([c.astype(BF16) for c in by_x], along_x)
    mine = total(by_x[0], arrived).T
    keep = lax.dynamic_slice_in_dim(mine, core * wrows, wrows, 0)
    got = permute(lax.dynamic_slice_in_dim(mine, (1 - core) * wrows, wrows, 0), SWAP)
    grad_weight = jnp.where(
        core == 0, jnp.concatenate([keep, got], 1), jnp.concatenate([got, keep], 1)
    )
    return (out, grad_tokens, grad_weight)


def solution(mesh):
    return jax.shard_map(
        per_device,
        mesh=mesh,
        in_specs=(
            P(("outer", "inner"), None),
            P(("outer", "inner"), None),
            P(("outer", "inner"), None),
            P(("outer", "inner"), None),
            P(("inner", "outer"), None),
            P(("inner", "outer"), None),
            P(("outer", "inner"), None),
        ),
        out_specs=(
            P(("outer", "inner"), None),
            P(("outer", "inner"), None),
            P(("inner", "outer"), None),
        ),
        check_vma=False,
    )
```

```python
import math

import jax
import jax.numpy as jnp
import numpy as np
from jax import lax
from jax.experimental import pallas as pl
from jax.experimental.pallas import tpu as pltpu
from jax.sharding import PartitionSpec as P

HD = 128
GROUP = 8
BLK = 512
AXES = ("outer", "inner")
F32 = jnp.float32
NT = (((1,), (1,)), ((), ()))
BF16 = jnp.bfloat16
VMEM_LIMIT = 48 * 1024 * 1024
ATTENTION_LIMIT = 40 * 1024 * 1024

INDEX = np.arange(128).reshape(2, 4, 2, 2, 4)


def permutation(move):
    pairs = []
    for zh in range(2):
        for x in range(4):
            for c in range(2):
                for zl in range(2):
                    for y in range(4):
                        nx, ny, nz, nc = move(x, y, zh * 2 + zl, c)
                        nx, ny, nz = nx % 4, ny % 4, nz % 4
                        target = INDEX[nz // 2, nx, nc, nz % 2, ny]
                        pairs.append((int(INDEX[zh, x, c, zl, y]), int(target)))
    return pairs


SWAP = permutation(lambda x, y, z, c: (x, y, z, 1 - c))


def along_x(d):
    return permutation(lambda x, y, z, c: (x + d, y, z, c))


def along_u(d):
    return permutation(lambda x, y, z, c: (x, y + d * (1 - c), z + d * c, c))


def along_v(d):
    return permutation(lambda x, y, z, c: (x, y + d * c, z + d * (1 - c), c))


def permute(a, perm):
    return lax.ppermute(a, AXES, perm)


def collect(a, along):
    two, right, left = (permute(a, along(d)) for d in (2, 1, -1))
    return [a, left, two, right]


def distribute(parts, along):
    return [permute(parts[2], along(2)), permute(parts[1], along(1)), permute(parts[3], along(-1))]


def params(**kw):
    return pltpu.CompilerParams(vmem_limit_bytes=VMEM_LIMIT, **kw)


def prepare(tokens, doc_ids):
    rows, width = tokens.shape
    steps = 4

    def kernel(tok_ref, doc_ref, inv_ref, bias_ref):
        i = pl.program_id(0)
        a = tok_ref[...].astype(F32)
        part = jnp.sum(a * a, axis=1, keepdims=True)

        @pl.when(i == 0)
        def _():
            row = jnp.broadcast_to(doc_ref[...].astype(F32), (rows, rows))
            s = lax.broadcasted_iota(jnp.int32, (rows, rows), 0)
            t = lax.broadcasted_iota(jnp.int32, (rows, rows), 1)
            bias_ref[...] = jnp.where((s <= t) & (row == row.T), 0.0, -1e30).astype(F32)
            inv_ref[...] = part

        @pl.when(i > 0)
        def _():
            inv_ref[...] += part

        @pl.when(i == steps - 1)
        def _():
            inv_ref[...] = lax.rsqrt(inv_ref[...] * (1.0 / width) + 1e-05)

    return pl.pallas_call(
        kernel,
        out_shape=(
            jax.ShapeDtypeStruct((rows, 1), F32),
            jax.ShapeDtypeStruct((rows, rows), F32),
        ),
        grid=(steps,),
        in_specs=[
            pl.BlockSpec((rows, width // steps), lambda i: (0, i)),
            pl.BlockSpec((1, rows), lambda i: (0, 0)),
        ],
        out_specs=(
            pl.BlockSpec((rows, 1), lambda i: (0, 0)),
            pl.BlockSpec((rows, rows), lambda i: (0, 0)),
        ),
        compiler_params=params(),
        cost_estimate=pl.CostEstimate(
            flops=rows * width * 3, bytes_accessed=rows * width * 2, transcendentals=0
        ),
        name="prepare",
    )(tokens, doc_ids)


def keys_part(order, own, sib, ws, acc, rvs):
    rows = own.shape[0]
    cols = ws[0].shape[-1]
    first = acc is None
    n = len(ws)

    def kernel(order_ref, *refs):
        tok_refs, w_refs = refs[:8], refs[8 : 8 + n]
        rest = refs[8 + n :]
        out_own, out_sib = rest[-2:]
        i = pl.program_id(0)
        x = jnp.concatenate(
            [jnp.concatenate([tok_refs[4 * s + k][...] for k in range(4)], 1) for s in range(2)], 0
        )

        def add(w, start):
            p = jnp.dot(x, w.reshape(4 * BLK, cols), preferred_element_type=F32)
            if start and first:
                out_own[...] = p[:rows]
                out_sib[...] = p[rows:]
            elif start:
                out_own[...] = rest[0][...] + p[:rows]
                out_sib[...] = rest[1][...] + p[rows:]
            else:
                out_own[...] += p[:rows]
                out_sib[...] += p[rows:]

        for k in range(n):

            @pl.when(i == k)
            def _(k=k):
                add(w_refs[k][...], k == 0)

    tok = [
        pl.BlockSpec((rows, BLK), lambda i, o, k=k: (0, o[(rvs[0] + i) * 4 + k])) for k in range(4)
    ]
    whole = pl.BlockSpec((rows, cols), lambda i, o: (0, 0))
    wspec = pl.BlockSpec((4, BLK, cols), lambda i, o: (0, 0, 0))
    out = jax.ShapeDtypeStruct((rows, cols), F32)
    return pl.pallas_call(
        kernel,
        out_shape=(out, out),
        grid_spec=pltpu.PrefetchScalarGridSpec(
            num_scalar_prefetch=1,
            grid=(n,),
            in_specs=tok + tok + [wspec] * n + ([] if first else [whole, whole]),
            out_specs=(whole, whole),
        ),
        compiler_params=params(),
        cost_estimate=pl.CostEstimate(
            flops=4 * n * rows * cols * BLK * 4,
            bytes_accessed=n * rows * BLK * 16,
            transcendentals=0,
        ),
        name="keys_part",
    )(order, *[own] * 4, *[sib] * 4, *ws, *(() if first else acc))


def attention(queries, keys_own, keys_oth, values, out_grad, inv, bias):
    rows = queries.shape[0]
    scale = HD ** (-0.5)
    cols = keys_own.shape[1]

    def kernel(q_ref, ko_ref, kt_ref, v_ref, g_ref, inv_ref, bias, *rest):
        o_ref, dk_ref, dwo_ref, dwt_ref, ms_ref, acc, kf = rest
        h = pl.program_id(0)
        core = lax.axis_index("outer") % 2
        is_own = h // 2 == core
        at = pl.ds(pl.multiple_of((h % 2) * HD, HD), HD)

        @pl.when(h == 0)
        def _():
            ms_ref[...] = jnp.zeros_like(ms_ref)

        @pl.when(is_own)
        def _():
            kf[...] = ko_ref[:, at] * inv_ref[...]

        @pl.when(jnp.logical_not(is_own))
        def _():
            kf[...] = kt_ref[:, at] * inv_ref[...]

        kb = (kf[...] * (scale * math.log2(math.e))).astype(BF16)
        vb = v_ref[...]
        vt = vb.astype(F32).T.astype(BF16)
        acc[...] = jnp.zeros_like(acc)

        def scores(j, part):
            n = (j + 1) * HD
            ts = slice(j * HD, n)
            cut = [slice(a * HD, (a + 1) * HD) for a in part]
            q = jnp.concatenate([q_ref[ts, c] for c in cut], axis=0)
            g = jnp.concatenate([g_ref[ts, c] for c in cut], axis=0)
            sc = lax.dot_general(kb[:n], q, NT, preferred_element_type=F32)
            return q, sc, lax.dot_general(vb[:n], g, NT, preferred_element_type=F32)

        def soften(j, part, sc, dp):
            n = (j + 1) * HD
            sc = sc + jnp.concatenate([bias[:n, j * HD : n]] * len(part), axis=1)
            top = jnp.max(sc, axis=0, keepdims=True)
            e = jnp.exp2(sc - top)
            p = e * (1.0 / jnp.sum(e, axis=0, keepdims=True))
            pd = p * dp
            ds = (pd - p * jnp.sum(pd, axis=0, keepdims=True)).astype(BF16)
            return p.astype(BF16), ds

        def finish(j, part, q, pb, ds):
            n = (j + 1) * HD
            ot = jnp.dot(vt[:, :n], pb, preferred_element_type=F32)
            o = ot.T.astype(BF16)
            for k, a in enumerate(part):
                o_ref[j * HD : n, a * HD : (a + 1) * HD] = o[k * HD : (k + 1) * HD]
            acc[:n] += jnp.dot(ds, q, preferred_element_type=F32)

        tiles = [(j, range(a, a + 4)) for j in (2, 1, 0) for a in (0, 4)]
        now = scores(*tiles[0])
        before = None
        for i, tile in enumerate(tiles):
            later = scores(*tiles[i + 1]) if i + 1 < len(tiles) else None
            q, sc, dp = now
            soft = soften(*tile, sc, dp)
            if before is not None:
                finish(*before)
            before = (*tile, q, *soft)
            now = later
        finish(*before)
        dk = acc[...] * scale
        dkb = dk.astype(BF16)
        dkw = (dk * inv_ref[...]).T.astype(BF16)
        ms_ref[...] += jnp.sum(dkb.astype(F32) * kf[...], axis=1, keepdims=True)

        @pl.when(is_own)
        def _():
            dk_ref[:, at] = dkb
            dwo_ref[at, :] = dkw

        @pl.when(jnp.logical_not(is_own))
        def _():
            dk_ref[:, pl.ds(pl.multiple_of((h % 2) * HD + cols, HD), HD)] = dkb
            dwt_ref[at, :] = dkw

    wide = pl.BlockSpec((rows, GROUP * HD), lambda h: (0, h))
    head = pl.BlockSpec((rows, HD), lambda h: (0, h))

    def whole(*shape):
        return pl.BlockSpec(shape, lambda h: (0, 0))

    half = whole(rows, cols)
    halft = whole(cols, rows)
    one = whole(rows, 1)
    return pl.pallas_call(
        kernel,
        out_shape=(
            jax.ShapeDtypeStruct(queries.shape, BF16),
            jax.ShapeDtypeStruct((rows, 2 * cols), BF16),
            jax.ShapeDtypeStruct((cols, rows), BF16),
            jax.ShapeDtypeStruct((cols, rows), BF16),
            jax.ShapeDtypeStruct((rows, 1), F32),
        ),
        grid=(4,),
        in_specs=[wide, half, half, head, wide, one, whole(rows, rows)],
        out_specs=(wide, whole(rows, 2 * cols), halft, halft, one),
        scratch_shapes=[pltpu.VMEM((rows, HD), F32), pltpu.VMEM((rows, HD), F32)],
        compiler_params=pltpu.CompilerParams(vmem_limit_bytes=ATTENTION_LIMIT),
        cost_estimate=pl.CostEstimate(
            flops=8 * 32 * rows * rows * HD * 2 // 3,
            bytes_accessed=rows * 4096 * 6,
            transcendentals=32 * rows * rows * 2 // 3,
        ),
        name="attention",
    )(queries, keys_own, keys_oth, values, out_grad, inv, bias)


def grad_part(order, own, sib, dk_own, dk_sib, rv):
    cols, rows = dk_own.shape

    def kernel(order_ref, *refs):
        a_ref, b_ref, out = refs[4:]
        dk = jnp.concatenate([a_ref[...], b_ref[...]], 1)
        for k in range(2):
            x = jnp.concatenate([refs[k][...], refs[2 + k][...]], 0)
            out[k] = jnp.dot(dk, x, preferred_element_type=F32).astype(BF16)

    tok = [
        pl.BlockSpec((rows, BLK), lambda i, o, k=k: (0, o[rv * 4 + 2 * i + k])) for k in range(2)
    ]
    half = pl.BlockSpec((cols, rows), lambda i, o: (0, 0))
    return pl.pallas_call(
        kernel,
        out_shape=jax.ShapeDtypeStruct((4, cols, BLK), BF16),
        grid_spec=pltpu.PrefetchScalarGridSpec(
            num_scalar_prefetch=1,
            grid=(2,),
            in_specs=tok + tok + [half, half],
            out_specs=pl.BlockSpec((2, cols, BLK), lambda i, o: (i, 0, 0)),
        ),
        compiler_params=params(),
        cost_estimate=pl.CostEstimate(
            flops=4 * rows * cols * BLK * 4, bytes_accessed=rows * BLK * 16, transcendentals=0
        ),
        name="grad_part",
    )(order, *[own] * 2, *[sib] * 2, dk_own, dk_sib)


def token_grad(place, tokens, dk, w_own, w_sib, inv, ms):
    rows, width = tokens.shape
    cols = w_own[0].shape[-1]
    step = 2

    def kernel(place_ref, tok_ref, dk_ref, *rest):
        own, sib = rest[:4], rest[4:8]
        inv_ref, ms_ref, out, w = rest[8:]
        i = pl.program_id(0)

        @pl.when(i == 0)
        def _():
            for k in range(4):
                w[4 * k : 4 * k + 4, :, :cols] = own[k][...]
            for k in range(4):
                for m in range(4):
                    w[4 * m + k, :, cols:] = sib[k][m]

        r = inv_ref[...]
        mean = ms_ref[...] * (r * r * (1.0 / width))
        for k in range(step):
            dn = lax.dot_general(
                dk_ref[...],
                w[place_ref[i * step + k]],
                NT,
                preferred_element_type=F32,
            )
            c = slice(k * BLK, (k + 1) * BLK)
            out[:, c] = (r * dn - tok_ref[:, c].astype(F32) * mean).astype(BF16)

    tok = pl.BlockSpec((rows, BLK * step), lambda i, o: (0, i))
    one = pl.BlockSpec((rows, 1), lambda i, o: (0, 0))
    wspec = pl.BlockSpec((4, BLK, cols), lambda i, o: (0, 0, 0))
    return pl.pallas_call(
        kernel,
        out_shape=jax.ShapeDtypeStruct(tokens.shape, BF16),
        grid_spec=pltpu.PrefetchScalarGridSpec(
            num_scalar_prefetch=1,
            grid=(16 // step,),
            in_specs=[tok, pl.BlockSpec((rows, 2 * cols), lambda i, o: (0, 0))]
            + [wspec] * 8
            + [one, one],
            out_specs=tok,
            scratch_shapes=[pltpu.VMEM((16, BLK, 2 * cols), BF16)],
        ),
        compiler_params=params(),
        cost_estimate=pl.CostEstimate(
            flops=4 * rows * cols * width, bytes_accessed=rows * width * 5, transcendentals=0
        ),
        name="token_grad",
    )(place, tokens, dk, *w_own, *w_sib, inv, ms)


def per_device(tokens, queries, values, doc_ids, weight_codes, weight_scales, out_grad):
    rows, width = tokens.shape
    outer, inner = lax.axis_index("outer"), lax.axis_index("inner")
    x, core, y = (outer // 2) % 4, outer % 2, inner % 4
    z = (outer // 8) * 2 + inner // 4
    u, v = jnp.where(core == 0, y, z), jnp.where(core == 0, z, y)
    ring4 = jnp.arange(4, dtype=jnp.int32)
    bv, bu = (v + ring4[:, None]) % 4, (u + ring4[None, :]) % 4
    by, bz = jnp.where(core == 0, bu, bv), jnp.where(core == 0, bv, bu)
    order = (((bz % 2) * 4 + by) * 2 + bz // 2).reshape(16).astype(jnp.int32)
    q = jnp.arange(16, dtype=jnp.int32)
    ry, rz = (q // 2 - y) % 4, ((q % 2) * 2 + q // 8 - z) % 4
    rv, ru = jnp.where(core == 0, rz, ry), jnp.where(core == 0, ry, rz)
    place = (rv * 4 + ru).astype(jnp.int32)

    factor = jnp.exp2(weight_scales.astype(F32))
    wrows, wcols = weight_codes.shape
    weight = weight_codes.astype(F32).reshape(2, wrows // 2, wcols) * factor[:, None, :]
    weight = weight.reshape(wrows, wcols).astype(BF16)
    hc = wcols // 2
    keep = jnp.where(core == 0, weight[:, :hc], weight[:, hc:])
    send = jnp.where(core == 0, weight[:, hc:], weight[:, :hc])
    got = permute(send, SWAP)
    chip = jnp.where(
        core == 0, jnp.concatenate([keep, got], 0), jnp.concatenate([got, keep], 0)
    )
    tokens_later, chip = lax.optimization_barrier((tokens, chip))
    tokens_sib = permute(tokens_later, SWAP)
    ring = collect(chip, along_x)
    ordered = []
    for i in range(4):
        r = (i - x) % 4
        ordered.append(
            jnp.where(r == 0, ring[0], jnp.where(r == 1, ring[1], jnp.where(r == 2, ring[2], ring[3])))
        )
    block = jnp.concatenate(ordered, 0)
    plane = jnp.stack(collect(block, along_u))
    plane, tokens_now, tokens_sib, order, place = lax.optimization_barrier(
        (plane, tokens, tokens_sib, order, place)
    )
    w_own = collect(plane, along_v)

    acc = keys_part(order, tokens, tokens_sib, w_own[:1], None, (0,))
    inv, bias = prepare(tokens_now, doc_ids)
    w_own[3], inv, bias, *acc = lax.optimization_barrier((w_own[3], inv, bias, *acc))
    acc = keys_part(order, tokens, tokens_sib, w_own[3:], acc, (3,))
    w_own[1], w_own[2], *acc = lax.optimization_barrier((w_own[1], w_own[2], *acc))
    keys_own, keys_sib = keys_part(order, tokens, tokens_sib, w_own[1:3], acc, (1, 2))
    keys_oth = permute(keys_sib, SWAP)
    w_sib = [permute(w, SWAP) for w in w_own]

    out, dk, dkw_own, dkw_oth, ms = attention(
        queries, keys_own, keys_oth, values, out_grad, inv, bias
    )
    dkw_oth, *w_sib = lax.optimization_barrier((dkw_oth, *w_sib))
    dkw_sib = permute(dkw_oth, SWAP)

    parts = [None] * 4
    for r in (2, 1, 3, 0):
        parts[r] = grad_part(order, tokens, tokens_sib, dkw_own, dkw_sib, r)
    arrived = distribute(parts, along_v)
    grad_tokens = token_grad(place, tokens, dk, w_own, w_sib, inv, ms)
    grad_tokens, parts[0], *arrived = lax.optimization_barrier((grad_tokens, parts[0], *arrived))

    def total(own, others):
        s = own.astype(F32)
        for o in others:
            s = s + o.astype(F32)
        return s

    chunk = [total(parts[0][r], [a[r] for a in arrived]) for r in range(4)]
    arrived = distribute([c.astype(BF16) for c in chunk], along_u)
    line = total(chunk[0], arrived)
    by_x = [lax.dynamic_slice_in_dim(line, ((x + r) % 4) * HD, HD, 1) for r in range(4)]
    arrived = distribute([c.astype(BF16) for c in by_x], along_x)
    mine = total(by_x[0], arrived).T
    keep = lax.dynamic_slice_in_dim(mine, core * wrows, wrows, 0)
    got = permute(lax.dynamic_slice_in_dim(mine, (1 - core) * wrows, wrows, 0), SWAP)
    grad_weight = jnp.where(
        core == 0, jnp.concatenate([keep, got], 1), jnp.concatenate([got, keep], 1)
    )
    return (out, grad_tokens, grad_weight)


def solution(mesh):
    return jax.shard_map(
        per_device,
        mesh=mesh,
        in_specs=(
            P(("outer", "inner"), None),
            P(("outer", "inner"), None),
            P(("outer", "inner"), None),
            P(("outer", "inner"), None),
            P(("inner", "outer"), None),
            P(("inner", "outer"), None),
            P(("outer", "inner"), None),
        ),
        out_specs=(
            P(("outer", "inner"), None),
            P(("outer", "inner"), None),
            P(("inner", "outer"), None),
        ),
        check_vma=False,
    )
```

```python
import math

import jax
import jax.numpy as jnp
import numpy as np
from jax import lax
from jax.experimental import pallas as pl
from jax.experimental.pallas import tpu as pltpu
from jax.sharding import PartitionSpec as P

HD = 128
GROUP = 8
BLK = 512
AXES = ("outer", "inner")
F32 = jnp.float32
NT = (((1,), (1,)), ((), ()))
BF16 = jnp.bfloat16
VMEM_LIMIT = 48 * 1024 * 1024
ATTENTION_LIMIT = 52 * 1024 * 1024

INDEX = np.arange(128).reshape(2, 4, 2, 2, 4)


def permutation(move):
    pairs = []
    for zh in range(2):
        for x in range(4):
            for c in range(2):
                for zl in range(2):
                    for y in range(4):
                        nx, ny, nz, nc = move(x, y, zh * 2 + zl, c)
                        nx, ny, nz = nx % 4, ny % 4, nz % 4
                        target = INDEX[nz // 2, nx, nc, nz % 2, ny]
                        pairs.append((int(INDEX[zh, x, c, zl, y]), int(target)))
    return pairs


SWAP = permutation(lambda x, y, z, c: (x, y, z, 1 - c))


def along_x(d):
    return permutation(lambda x, y, z, c: (x + d, y, z, c))


def along_u(d):
    return permutation(lambda x, y, z, c: (x, y + d * (1 - c), z + d * c, c))


def along_v(d):
    return permutation(lambda x, y, z, c: (x, y + d * c, z + d * (1 - c), c))


def permute(a, perm):
    return lax.ppermute(a, AXES, perm)


def collect(a, along):
    two, right, left = lax.optimization_barrier(
        tuple(permute(a, along(d)) for d in (2, 1, -1))
    )
    return [a, left, two, right]


def distribute(parts, along):
    return [permute(parts[2], along(2)), permute(parts[1], along(1)), permute(parts[3], along(-1))]


def params(**kw):
    return pltpu.CompilerParams(vmem_limit_bytes=VMEM_LIMIT, **kw)


def prepare(tokens, doc_ids):
    rows, width = tokens.shape
    steps = 4

    def kernel(tok_ref, doc_ref, inv_ref, bias_ref):
        i = pl.program_id(0)
        a = tok_ref[...].astype(F32)
        part = jnp.sum(a * a, axis=1, keepdims=True)

        @pl.when(i == 0)
        def _():
            row = jnp.broadcast_to(doc_ref[...].astype(F32), (rows, rows))
            s = lax.broadcasted_iota(jnp.int32, (rows, rows), 0)
            t = lax.broadcasted_iota(jnp.int32, (rows, rows), 1)
            bias_ref[...] = jnp.where((s <= t) & (row == row.T), 0.0, -1e30).astype(F32)
            inv_ref[...] = part

        @pl.when(i > 0)
        def _():
            inv_ref[...] += part

        @pl.when(i == steps - 1)
        def _():
            inv_ref[...] = lax.rsqrt(inv_ref[...] * (1.0 / width) + 1e-05)

    return pl.pallas_call(
        kernel,
        out_shape=(
            jax.ShapeDtypeStruct((rows, 1), F32),
            jax.ShapeDtypeStruct((rows, rows), F32),
        ),
        grid=(steps,),
        in_specs=[
            pl.BlockSpec((rows, width // steps), lambda i: (0, i)),
            pl.BlockSpec((1, rows), lambda i: (0, 0)),
        ],
        out_specs=(
            pl.BlockSpec((rows, 1), lambda i: (0, 0)),
            pl.BlockSpec((rows, rows), lambda i: (0, 0)),
        ),
        compiler_params=params(),
        cost_estimate=pl.CostEstimate(
            flops=rows * width * 3, bytes_accessed=rows * width * 2, transcendentals=0
        ),
        name="prepare",
    )(tokens, doc_ids)


def keys_part(order, own, sib, ws, acc, rvs):
    rows = own.shape[0]
    cols = ws[0].shape[-1]
    first = acc is None
    n = len(ws)
    by = rvs[1] - rvs[0] if n > 1 else 0

    def kernel(order_ref, *refs):
        tok_refs, w_refs = refs[:8], refs[8 : 8 + n]
        rest = refs[8 + n :]
        out_own, out_sib = rest[-2:]
        i = pl.program_id(0)
        x = jnp.concatenate(
            [jnp.concatenate([tok_refs[4 * s + k][...] for k in range(4)], 1) for s in range(2)], 0
        )

        def add(w, start):
            p = jnp.dot(x, w.reshape(4 * BLK, cols), preferred_element_type=F32)
            if start and first:
                out_own[...] = p[:rows]
                out_sib[...] = p[rows:]
            elif start:
                out_own[...] = rest[0][...] + p[:rows]
                out_sib[...] = rest[1][...] + p[rows:]
            else:
                out_own[...] += p[:rows]
                out_sib[...] += p[rows:]

        for k in range(n):

            @pl.when(i == k)
            def _(k=k):
                add(w_refs[k][...], k == 0)

    tok = [
        pl.BlockSpec((rows, BLK), lambda i, o, k=k: (0, o[(rvs[0] + by * i) * 4 + k])) for k in range(4)
    ]
    whole = pl.BlockSpec((rows, cols), lambda i, o: (0, 0))
    wspec = pl.BlockSpec((4, BLK, cols), lambda i, o: (0, 0, 0))
    out = jax.ShapeDtypeStruct((rows, cols), F32)
    return pl.pallas_call(
        kernel,
        out_shape=(out, out),
        grid_spec=pltpu.PrefetchScalarGridSpec(
            num_scalar_prefetch=1,
            grid=(n,),
            in_specs=tok + tok + [wspec] * n + ([] if first else [whole, whole]),
            out_specs=(whole, whole),
        ),
        compiler_params=params(),
        cost_estimate=pl.CostEstimate(
            flops=4 * n * rows * cols * BLK * 4,
            bytes_accessed=n * rows * BLK * 16,
            transcendentals=0,
        ),
        name="keys_part",
    )(order, *[own] * 4, *[sib] * 4, *ws, *(() if first else acc))


def attention(queries, keys_own, keys_oth, values, out_grad, inv, bias):
    rows = queries.shape[0]
    scale = HD ** (-0.5)
    cols = keys_own.shape[1]

    def kernel(q_ref, ko_ref, kt_ref, v_ref, g_ref, inv_ref, bias, *rest):
        o_ref, dk_ref, dwo_ref, dwt_ref, ms_ref, acc, kf = rest
        h = pl.program_id(0)
        core = lax.axis_index("outer") % 2
        is_own = h // 2 == core
        at = pl.ds(pl.multiple_of((h % 2) * HD, HD), HD)

        @pl.when(h == 0)
        def _():
            ms_ref[...] = jnp.zeros_like(ms_ref)

        @pl.when(is_own)
        def _():
            kf[...] = ko_ref[:, at] * inv_ref[...]

        @pl.when(jnp.logical_not(is_own))
        def _():
            kf[...] = kt_ref[:, at] * inv_ref[...]

        kb = (kf[...] * (scale * math.log2(math.e))).astype(BF16)
        vb = v_ref[...]
        vt = vb.astype(F32).T.astype(BF16)
        acc[...] = jnp.zeros_like(acc)

        def scores(j, part):
            n = (j + 1) * HD
            ts = slice(j * HD, n)
            cut = [slice(a * HD, (a + 1) * HD) for a in part]
            q = jnp.concatenate([q_ref[ts, c] for c in cut], axis=0)
            g = jnp.concatenate([g_ref[ts, c] for c in cut], axis=0)
            sc = lax.dot_general(kb[:n], q, NT, preferred_element_type=F32)
            return q, sc, lax.dot_general(vb[:n], g, NT, preferred_element_type=F32)

        def soften(j, part, sc, dp):
            n = (j + 1) * HD
            sc = sc + jnp.concatenate([bias[:n, j * HD : n]] * len(part), axis=1)
            top = jnp.max(sc, axis=0, keepdims=True)
            e = jnp.exp2(sc - top)
            p = e * (1.0 / jnp.sum(e, axis=0, keepdims=True))
            pd = p * dp
            ds = (pd - p * jnp.sum(pd, axis=0, keepdims=True)).astype(BF16)
            return p.astype(BF16), ds

        def finish(j, part, q, pb, ds):
            n = (j + 1) * HD
            ot = jnp.dot(vt[:, :n], pb, preferred_element_type=F32)
            o = ot.T.astype(BF16)
            for k, a in enumerate(part):
                o_ref[j * HD : n, a * HD : (a + 1) * HD] = o[k * HD : (k + 1) * HD]
            acc[:n] += jnp.dot(ds, q, preferred_element_type=F32)

        tiles = [(j, range(a, a + 4)) for j in (2, 1, 0) for a in (0, 4)]
        now = scores(*tiles[0])
        before = None
        for i, tile in enumerate(tiles):
            later = scores(*tiles[i + 1]) if i + 1 < len(tiles) else None
            q, sc, dp = now
            soft = soften(*tile, sc, dp)
            if before is not None:
                finish(*before)
            before = (*tile, q, *soft)
            now = later
        finish(*before)
        dk = acc[...] * scale
        dkb = dk.astype(BF16)
        dkw = (dk * inv_ref[...]).T.astype(BF16)
        ms_ref[...] += jnp.sum(dkb.astype(F32) * kf[...], axis=1, keepdims=True)

        @pl.when(is_own)
        def _():
            dk_ref[:, at] = dkb
            dwo_ref[at, :] = dkw

        @pl.when(jnp.logical_not(is_own))
        def _():
            dk_ref[:, pl.ds(pl.multiple_of((h % 2) * HD + cols, HD), HD)] = dkb
            dwt_ref[at, :] = dkw

    wide = pl.BlockSpec((rows, GROUP * HD), lambda h: (0, h))
    head = pl.BlockSpec((rows, HD), lambda h: (0, h))

    def whole(*shape):
        return pl.BlockSpec(shape, lambda h: (0, 0))

    half = whole(rows, cols)
    halft = whole(cols, rows)
    one = whole(rows, 1)
    return pl.pallas_call(
        kernel,
        out_shape=(
            jax.ShapeDtypeStruct(queries.shape, BF16),
            jax.ShapeDtypeStruct((rows, 2 * cols), BF16),
            jax.ShapeDtypeStruct((cols, rows), BF16),
            jax.ShapeDtypeStruct((cols, rows), BF16),
            jax.ShapeDtypeStruct((rows, 1), F32),
        ),
        grid=(4,),
        in_specs=[wide, half, half, head, wide, one, whole(rows, rows)],
        out_specs=(wide, whole(rows, 2 * cols), halft, halft, one),
        scratch_shapes=[pltpu.VMEM((rows, HD), F32), pltpu.VMEM((rows, HD), F32)],
        compiler_params=pltpu.CompilerParams(vmem_limit_bytes=ATTENTION_LIMIT),
        cost_estimate=pl.CostEstimate(
            flops=8 * 32 * rows * rows * HD * 2 // 3,
            bytes_accessed=rows * 4096 * 6,
            transcendentals=32 * rows * rows * 2 // 3,
        ),
        name="attention",
    )(queries, keys_own, keys_oth, values, out_grad, inv, bias)


def grad_part(order, own, sib, dk_own, dk_sib, rv):
    cols, rows = dk_own.shape

    def kernel(order_ref, *refs):
        a_ref, b_ref, out = refs[4:]
        dk = jnp.concatenate([a_ref[...], b_ref[...]], 1)
        for k in range(2):
            x = jnp.concatenate([refs[k][...], refs[2 + k][...]], 0)
            out[k] = jnp.dot(dk, x, preferred_element_type=F32).astype(BF16)

    tok = [
        pl.BlockSpec((rows, BLK), lambda i, o, k=k: (0, o[rv * 4 + 2 * i + k])) for k in range(2)
    ]
    half = pl.BlockSpec((cols, rows), lambda i, o: (0, 0))
    return pl.pallas_call(
        kernel,
        out_shape=jax.ShapeDtypeStruct((4, cols, BLK), BF16),
        grid_spec=pltpu.PrefetchScalarGridSpec(
            num_scalar_prefetch=1,
            grid=(2,),
            in_specs=tok + tok + [half, half],
            out_specs=pl.BlockSpec((2, cols, BLK), lambda i, o: (i, 0, 0)),
        ),
        compiler_params=params(),
        cost_estimate=pl.CostEstimate(
            flops=4 * rows * cols * BLK * 4, bytes_accessed=rows * BLK * 16, transcendentals=0
        ),
        name="grad_part",
    )(order, *[own] * 2, *[sib] * 2, dk_own, dk_sib)


def token_grad(place, tokens, dk, w_own, w_sib, inv, ms):
    rows, width = tokens.shape
    cols = w_own[0].shape[-1]
    step = 2

    def kernel(place_ref, tok_ref, dk_ref, *rest):
        own, sib = rest[:4], rest[4:8]
        inv_ref, ms_ref, out, w = rest[8:]
        i = pl.program_id(0)

        @pl.when(i == 0)
        def _():
            for k in range(4):
                w[4 * k : 4 * k + 4, :, :cols] = own[k][...]
            for k in range(4):
                for m in range(4):
                    w[4 * m + k, :, cols:] = sib[k][m]

        r = inv_ref[...]
        mean = ms_ref[...] * (r * r * (1.0 / width))
        for k in range(step):
            dn = lax.dot_general(
                dk_ref[...],
                w[place_ref[i * step + k]],
                NT,
                preferred_element_type=F32,
            )
            c = slice(k * BLK, (k + 1) * BLK)
            out[:, c] = (r * dn - tok_ref[:, c].astype(F32) * mean).astype(BF16)

    tok = pl.BlockSpec((rows, BLK * step), lambda i, o: (0, i))
    one = pl.BlockSpec((rows, 1), lambda i, o: (0, 0))
    wspec = pl.BlockSpec((4, BLK, cols), lambda i, o: (0, 0, 0))
    return pl.pallas_call(
        kernel,
        out_shape=jax.ShapeDtypeStruct(tokens.shape, BF16),
        grid_spec=pltpu.PrefetchScalarGridSpec(
            num_scalar_prefetch=1,
            grid=(16 // step,),
            in_specs=[tok, pl.BlockSpec((rows, 2 * cols), lambda i, o: (0, 0))]
            + [wspec] * 8
            + [one, one],
            out_specs=tok,
            scratch_shapes=[pltpu.VMEM((16, BLK, 2 * cols), BF16)],
        ),
        compiler_params=params(),
        cost_estimate=pl.CostEstimate(
            flops=4 * rows * cols * width, bytes_accessed=rows * width * 5, transcendentals=0
        ),
        name="token_grad",
    )(place, tokens, dk, *w_own, *w_sib, inv, ms)


def per_device(tokens, queries, values, doc_ids, weight_codes, weight_scales, out_grad):
    rows, width = tokens.shape
    outer, inner = lax.axis_index("outer"), lax.axis_index("inner")
    x, core, y = (outer // 2) % 4, outer % 2, inner % 4
    z = (outer // 8) * 2 + inner // 4
    u, v = jnp.where(core == 0, y, z), jnp.where(core == 0, z, y)
    ring4 = jnp.arange(4, dtype=jnp.int32)
    bv, bu = (v + ring4[:, None]) % 4, (u + ring4[None, :]) % 4
    by, bz = jnp.where(core == 0, bu, bv), jnp.where(core == 0, bv, bu)
    order = (((bz % 2) * 4 + by) * 2 + bz // 2).reshape(16).astype(jnp.int32)
    q = jnp.arange(16, dtype=jnp.int32)
    ry, rz = (q // 2 - y) % 4, ((q % 2) * 2 + q // 8 - z) % 4
    rv, ru = jnp.where(core == 0, rz, ry), jnp.where(core == 0, ry, rz)
    place = (rv * 4 + ru).astype(jnp.int32)

    factor = jnp.exp2(weight_scales.astype(F32))
    wrows, wcols = weight_codes.shape
    weight = weight_codes.astype(F32).reshape(2, wrows // 2, wcols) * factor[:, None, :]
    weight = weight.reshape(wrows, wcols).astype(BF16)
    hc = wcols // 2
    keep = jnp.where(core == 0, weight[:, :hc], weight[:, hc:])
    send = jnp.where(core == 0, weight[:, hc:], weight[:, :hc])
    got = permute(send, SWAP)
    chip = jnp.where(
        core == 0, jnp.concatenate([keep, got], 0), jnp.concatenate([got, keep], 0)
    )
    tokens_later, chip = lax.optimization_barrier((tokens, chip))
    tokens_sib = permute(tokens_later, SWAP)
    ring = collect(chip, along_x)
    ordered = []
    for i in range(4):
        r = (i - x) % 4
        ordered.append(
            jnp.where(r == 0, ring[0], jnp.where(r == 1, ring[1], jnp.where(r == 2, ring[2], ring[3])))
        )
    block = jnp.concatenate(ordered, 0)
    plane = jnp.stack(collect(block, along_u))
    plane, tokens_now, tokens_sib, order, place = lax.optimization_barrier(
        (plane, tokens, tokens_sib, order, place)
    )
    w_own = [plane] + [permute(plane, along_v(d)) for d in (-1, 2, 1)]

    acc = keys_part(order, tokens, tokens_sib, w_own[:1], None, (0,))
    inv, bias = prepare(tokens_now, doc_ids)
    w_own[2], inv, bias, *acc = lax.optimization_barrier((w_own[2], inv, bias, *acc))
    acc = keys_part(order, tokens, tokens_sib, w_own[2:3], acc, (2,))
    w_own[3], w_own[1], *acc = lax.optimization_barrier((w_own[3], w_own[1], *acc))
    keys_own, keys_sib = keys_part(order, tokens, tokens_sib, w_own[1::2], acc, (1, 3))
    keys_oth = permute(keys_sib, SWAP)
    w_sib = [permute(w, SWAP) for w in w_own]

    out, dk, dkw_own, dkw_oth, ms = attention(
        queries, keys_own, keys_oth, values, out_grad, inv, bias
    )
    dkw_oth, *w_sib = lax.optimization_barrier((dkw_oth, *w_sib))
    dkw_sib = permute(dkw_oth, SWAP)

    parts = [None] * 4
    for r in (2, 1, 3, 0):
        parts[r] = grad_part(order, tokens, tokens_sib, dkw_own, dkw_sib, r)
    arrived = distribute(parts, along_v)
    grad_tokens = token_grad(place, tokens, dk, w_own, w_sib, inv, ms)
    grad_tokens, parts[0], *arrived = lax.optimization_barrier((grad_tokens, parts[0], *arrived))

    def total(own, others):
        s = own.astype(F32)
        for o in others:
            s = s + o.astype(F32)
        return s

    chunk = [total(parts[0][r], [a[r] for a in arrived]) for r in range(4)]
    arrived = distribute([c.astype(BF16) for c in chunk], along_u)
    line = total(chunk[0], arrived)
    by_x = [lax.dynamic_slice_in_dim(line, ((x + r) % 4) * HD, HD, 1) for r in range(4)]
    arrived = distribute([c.astype(BF16) for c in by_x], along_x)
    mine = total(by_x[0], arrived).T
    keep = lax.dynamic_slice_in_dim(mine, core * wrows, wrows, 0)
    got = permute(lax.dynamic_slice_in_dim(mine, (1 - core) * wrows, wrows, 0), SWAP)
    grad_weight = jnp.where(
        core == 0, jnp.concatenate([keep, got], 1), jnp.concatenate([got, keep], 1)
    )
    return (out, grad_tokens, grad_weight)


def solution(mesh):
    return jax.shard_map(
        per_device,
        mesh=mesh,
        in_specs=(
            P(("outer", "inner"), None),
            P(("outer", "inner"), None),
            P(("outer", "inner"), None),
            P(("outer", "inner"), None),
            P(("inner", "outer"), None),
            P(("inner", "outer"), None),
            P(("outer", "inner"), None),
        ),
        out_specs=(
            P(("outer", "inner"), None),
            P(("outer", "inner"), None),
            P(("inner", "outer"), None),
        ),
        check_vma=False,
    )
```

```python
import math

import jax
import jax.numpy as jnp
import numpy as np
from jax import lax
from jax.experimental import pallas as pl
from jax.experimental.pallas import tpu as pltpu
from jax.sharding import PartitionSpec as P

HD = 128
GROUP = 8
BLK = 512
AXES = ("outer", "inner")
F32 = jnp.float32
NT = (((1,), (1,)), ((), ()))
BF16 = jnp.bfloat16
VMEM_LIMIT = 48 * 1024 * 1024
ATTENTION_LIMIT = 52 * 1024 * 1024

INDEX = np.arange(128).reshape(2, 4, 2, 2, 4)


def permutation(move):
    pairs = []
    for zh in range(2):
        for x in range(4):
            for c in range(2):
                for zl in range(2):
                    for y in range(4):
                        nx, ny, nz, nc = move(x, y, zh * 2 + zl, c)
                        nx, ny, nz = nx % 4, ny % 4, nz % 4
                        target = INDEX[nz // 2, nx, nc, nz % 2, ny]
                        pairs.append((int(INDEX[zh, x, c, zl, y]), int(target)))
    return pairs


SWAP = permutation(lambda x, y, z, c: (x, y, z, 1 - c))


def along_x(d):
    return permutation(lambda x, y, z, c: (x + d, y, z, c))


def along_u(d):
    return permutation(lambda x, y, z, c: (x, y + d * (1 - c), z + d * c, c))


def along_v(d):
    return permutation(lambda x, y, z, c: (x, y + d * c, z + d * (1 - c), c))


def permute(a, perm):
    return lax.ppermute(a, AXES, perm)


def collect(a, along):
    two, right, left = lax.optimization_barrier(
        tuple(permute(a, along(d)) for d in (2, 1, -1))
    )
    return [a, left, two, right]


def distribute(parts, along):
    return [permute(parts[2], along(2)), permute(parts[1], along(1)), permute(parts[3], along(-1))]


def params(**kw):
    return pltpu.CompilerParams(vmem_limit_bytes=VMEM_LIMIT, **kw)


def prepare(tokens, doc_ids):
    rows, width = tokens.shape
    steps = 4

    def kernel(tok_ref, doc_ref, inv_ref, bias_ref):
        i = pl.program_id(0)
        a = tok_ref[...].astype(F32)
        part = jnp.sum(a * a, axis=1, keepdims=True)

        @pl.when(i == 0)
        def _():
            row = jnp.broadcast_to(doc_ref[...].astype(F32), (rows, rows))
            s = lax.broadcasted_iota(jnp.int32, (rows, rows), 0)
            t = lax.broadcasted_iota(jnp.int32, (rows, rows), 1)
            bias_ref[...] = jnp.where((s <= t) & (row == row.T), 0.0, -1e30).astype(F32)
            inv_ref[...] = part

        @pl.when(i > 0)
        def _():
            inv_ref[...] += part

        @pl.when(i == steps - 1)
        def _():
            inv_ref[...] = lax.rsqrt(inv_ref[...] * (1.0 / width) + 1e-05)

    return pl.pallas_call(
        kernel,
        out_shape=(
            jax.ShapeDtypeStruct((rows, 1), F32),
            jax.ShapeDtypeStruct((rows, rows), F32),
        ),
        grid=(steps,),
        in_specs=[
            pl.BlockSpec((rows, width // steps), lambda i: (0, i)),
            pl.BlockSpec((1, rows), lambda i: (0, 0)),
        ],
        out_specs=(
            pl.BlockSpec((rows, 1), lambda i: (0, 0)),
            pl.BlockSpec((rows, rows), lambda i: (0, 0)),
        ),
        compiler_params=params(),
        cost_estimate=pl.CostEstimate(
            flops=rows * width * 3, bytes_accessed=rows * width * 2, transcendentals=0
        ),
        name="prepare",
    )(tokens, doc_ids)


def keys_part(order, own, sib, ws, acc, rvs):
    rows = own.shape[0]
    cols = ws[0].shape[-1]
    first = acc is None
    n = len(ws)
    by = rvs[1] - rvs[0] if n > 1 else 0

    def kernel(order_ref, *refs):
        tok_refs, w_refs = refs[:8], refs[8 : 8 + n]
        rest = refs[8 + n :]
        out_own, out_sib = rest[-2:]
        i = pl.program_id(0)
        x = jnp.concatenate(
            [jnp.concatenate([tok_refs[4 * s + k][...] for k in range(4)], 1) for s in range(2)], 0
        )

        def add(w, start):
            p = jnp.dot(x, w.reshape(4 * BLK, cols), preferred_element_type=F32)
            if start and first:
                out_own[...] = p[:rows]
                out_sib[...] = p[rows:]
            elif start:
                out_own[...] = rest[0][...] + p[:rows]
                out_sib[...] = rest[1][...] + p[rows:]
            else:
                out_own[...] += p[:rows]
                out_sib[...] += p[rows:]

        for k in range(n):

            @pl.when(i == k)
            def _(k=k):
                add(w_refs[k][...], k == 0)

    tok = [
        pl.BlockSpec((rows, BLK), lambda i, o, k=k: (0, o[(rvs[0] + by * i) * 4 + k])) for k in range(4)
    ]
    whole = pl.BlockSpec((rows, cols), lambda i, o: (0, 0))
    wspec = pl.BlockSpec((4, BLK, cols), lambda i, o: (0, 0, 0))
    out = jax.ShapeDtypeStruct((rows, cols), F32)
    return pl.pallas_call(
        kernel,
        out_shape=(out, out),
        grid_spec=pltpu.PrefetchScalarGridSpec(
            num_scalar_prefetch=1,
            grid=(n,),
            in_specs=tok + tok + [wspec] * n + ([] if first else [whole, whole]),
            out_specs=(whole, whole),
        ),
        compiler_params=params(),
        cost_estimate=pl.CostEstimate(
            flops=4 * n * rows * cols * BLK * 4,
            bytes_accessed=n * rows * BLK * 16,
            transcendentals=0,
        ),
        name="keys_part",
    )(order, *[own] * 4, *[sib] * 4, *ws, *(() if first else acc))


def attention(queries, keys_own, keys_oth, values, out_grad, inv, bias):
    rows = queries.shape[0]
    scale = HD ** (-0.5)
    cols = keys_own.shape[1]

    def kernel(q_ref, ko_ref, kt_ref, v_ref, g_ref, inv_ref, bias, *rest):
        o_ref, dk_ref, dwo_ref, dwt_ref, ms_ref, acc, kf = rest
        h = pl.program_id(0)
        core = lax.axis_index("outer") % 2
        is_own = h // 2 == core
        at = pl.ds(pl.multiple_of((h % 2) * HD, HD), HD)

        @pl.when(h == 0)
        def _():
            ms_ref[...] = jnp.zeros_like(ms_ref)

        @pl.when(is_own)
        def _():
            kf[...] = ko_ref[:, at] * inv_ref[...]

        @pl.when(jnp.logical_not(is_own))
        def _():
            kf[...] = kt_ref[:, at] * inv_ref[...]

        kb = (kf[...] * (scale * math.log2(math.e))).astype(BF16)
        vb = v_ref[...]
        vt = vb.astype(F32).T.astype(BF16)
        acc[...] = jnp.zeros_like(acc)

        def scores(j, part):
            n = (j + 1) * HD
            ts = slice(j * HD, n)
            cut = [slice(a * HD, (a + 1) * HD) for a in part]
            q = jnp.concatenate([q_ref[ts, c] for c in cut], axis=0)
            g = jnp.concatenate([g_ref[ts, c] for c in cut], axis=0)
            sc = lax.dot_general(kb[:n], q, NT, preferred_element_type=F32)
            return q, sc, lax.dot_general(vb[:n], g, NT, preferred_element_type=F32)

        def soften(j, part, sc, dp):
            n = (j + 1) * HD
            sc = sc + jnp.concatenate([bias[:n, j * HD : n]] * len(part), axis=1)
            top = jnp.max(sc, axis=0, keepdims=True)
            e = jnp.exp2(sc - top)
            p = e * (1.0 / jnp.sum(e, axis=0, keepdims=True))
            pd = p * dp
            ds = (pd - p * jnp.sum(pd, axis=0, keepdims=True)).astype(BF16)
            return p.astype(BF16), ds

        def finish(j, part, q, pb, ds):
            n = (j + 1) * HD
            ot = jnp.dot(vt[:, :n], pb, preferred_element_type=F32)
            o = ot.T.astype(BF16)
            for k, a in enumerate(part):
                o_ref[j * HD : n, a * HD : (a + 1) * HD] = o[k * HD : (k + 1) * HD]
            acc[:n] += jnp.dot(ds, q, preferred_element_type=F32)

        tiles = [(j, range(a, a + 4)) for j in (2, 1, 0) for a in (0, 4)]
        now = scores(*tiles[0])
        before = None
        for i, tile in enumerate(tiles):
            later = scores(*tiles[i + 1]) if i + 1 < len(tiles) else None
            q, sc, dp = now
            soft = soften(*tile, sc, dp)
            if before is not None:
                finish(*before)
            before = (*tile, q, *soft)
            now = later
        finish(*before)
        dk = acc[...] * scale
        dkb = dk.astype(BF16)
        dkw = (dk * inv_ref[...]).T.astype(BF16)
        ms_ref[...] += jnp.sum(dkb.astype(F32) * kf[...], axis=1, keepdims=True)

        @pl.when(is_own)
        def _():
            dk_ref[:, at] = dkb
            dwo_ref[at, :] = dkw

        @pl.when(jnp.logical_not(is_own))
        def _():
            dk_ref[:, pl.ds(pl.multiple_of((h % 2) * HD + cols, HD), HD)] = dkb
            dwt_ref[at, :] = dkw

    wide = pl.BlockSpec((rows, GROUP * HD), lambda h: (0, h))
    head = pl.BlockSpec((rows, HD), lambda h: (0, h))

    def whole(*shape):
        return pl.BlockSpec(shape, lambda h: (0, 0))

    half = whole(rows, cols)
    halft = whole(cols, rows)
    one = whole(rows, 1)
    return pl.pallas_call(
        kernel,
        out_shape=(
            jax.ShapeDtypeStruct(queries.shape, BF16),
            jax.ShapeDtypeStruct((rows, 2 * cols), BF16),
            jax.ShapeDtypeStruct((cols, rows), BF16),
            jax.ShapeDtypeStruct((cols, rows), BF16),
            jax.ShapeDtypeStruct((rows, 1), F32),
        ),
        grid=(4,),
        in_specs=[wide, half, half, head, wide, one, whole(rows, rows)],
        out_specs=(wide, whole(rows, 2 * cols), halft, halft, one),
        scratch_shapes=[pltpu.VMEM((rows, HD), F32), pltpu.VMEM((rows, HD), F32)],
        compiler_params=pltpu.CompilerParams(vmem_limit_bytes=ATTENTION_LIMIT),
        cost_estimate=pl.CostEstimate(
            flops=8 * 32 * rows * rows * HD * 2 // 3,
            bytes_accessed=rows * 4096 * 6,
            transcendentals=32 * rows * rows * 2 // 3,
        ),
        name="attention",
    )(queries, keys_own, keys_oth, values, out_grad, inv, bias)


def grad_part(order, own, sib, dk_own, dk_sib, rv):
    cols, rows = dk_own.shape

    def kernel(order_ref, *refs):
        a_ref, b_ref, out = refs[4:]
        dk = jnp.concatenate([a_ref[...], b_ref[...]], 1)
        for k in range(2):
            x = jnp.concatenate([refs[k][...], refs[2 + k][...]], 0)
            out[k] = jnp.dot(dk, x, preferred_element_type=F32).astype(BF16)

    tok = [
        pl.BlockSpec((rows, BLK), lambda i, o, k=k: (0, o[rv * 4 + 2 * i + k])) for k in range(2)
    ]
    half = pl.BlockSpec((cols, rows), lambda i, o: (0, 0))
    return pl.pallas_call(
        kernel,
        out_shape=jax.ShapeDtypeStruct((4, cols, BLK), BF16),
        grid_spec=pltpu.PrefetchScalarGridSpec(
            num_scalar_prefetch=1,
            grid=(2,),
            in_specs=tok + tok + [half, half],
            out_specs=pl.BlockSpec((2, cols, BLK), lambda i, o: (i, 0, 0)),
        ),
        compiler_params=params(),
        cost_estimate=pl.CostEstimate(
            flops=4 * rows * cols * BLK * 4, bytes_accessed=rows * BLK * 16, transcendentals=0
        ),
        name="grad_part",
    )(order, *[own] * 2, *[sib] * 2, dk_own, dk_sib)


def token_grad(place, tokens, dk, w_own, w_sib, inv, ms):
    rows, width = tokens.shape
    cols = w_own[0].shape[-1]
    step = 2

    def kernel(place_ref, tok_ref, dk_ref, *rest):
        own, sib = rest[:4], rest[4:8]
        inv_ref, ms_ref, out, w = rest[8:]
        i = pl.program_id(0)

        @pl.when(i == 0)
        def _():
            for k in range(4):
                w[4 * k : 4 * k + 4, :, :cols] = own[k][...]
            for k in range(4):
                for m in range(4):
                    w[4 * m + k, :, cols:] = sib[k][m]

        r = inv_ref[...]
        mean = ms_ref[...] * (r * r * (1.0 / width))
        for k in range(step):
            dn = lax.dot_general(
                dk_ref[...],
                w[place_ref[i * step + k]],
                NT,
                preferred_element_type=F32,
            )
            c = slice(k * BLK, (k + 1) * BLK)
            out[:, c] = (r * dn - tok_ref[:, c].astype(F32) * mean).astype(BF16)

    tok = pl.BlockSpec((rows, BLK * step), lambda i, o: (0, i))
    one = pl.BlockSpec((rows, 1), lambda i, o: (0, 0))
    wspec = pl.BlockSpec((4, BLK, cols), lambda i, o: (0, 0, 0))
    return pl.pallas_call(
        kernel,
        out_shape=jax.ShapeDtypeStruct(tokens.shape, BF16),
        grid_spec=pltpu.PrefetchScalarGridSpec(
            num_scalar_prefetch=1,
            grid=(16 // step,),
            in_specs=[tok, pl.BlockSpec((rows, 2 * cols), lambda i, o: (0, 0))]
            + [wspec] * 8
            + [one, one],
            out_specs=tok,
            scratch_shapes=[pltpu.VMEM((16, BLK, 2 * cols), BF16)],
        ),
        compiler_params=params(),
        cost_estimate=pl.CostEstimate(
            flops=4 * rows * cols * width, bytes_accessed=rows * width * 5, transcendentals=0
        ),
        name="token_grad",
    )(place, tokens, dk, *w_own, *w_sib, inv, ms)


def per_device(tokens, queries, values, doc_ids, weight_codes, weight_scales, out_grad):
    rows, width = tokens.shape
    outer, inner = lax.axis_index("outer"), lax.axis_index("inner")
    x, core, y = (outer // 2) % 4, outer % 2, inner % 4
    z = (outer // 8) * 2 + inner // 4
    u, v = jnp.where(core == 0, y, z), jnp.where(core == 0, z, y)
    ring4 = jnp.arange(4, dtype=jnp.int32)
    bv, bu = (v + ring4[:, None]) % 4, (u + ring4[None, :]) % 4
    by, bz = jnp.where(core == 0, bu, bv), jnp.where(core == 0, bv, bu)
    order = (((bz % 2) * 4 + by) * 2 + bz // 2).reshape(16).astype(jnp.int32)
    q = jnp.arange(16, dtype=jnp.int32)
    ry, rz = (q // 2 - y) % 4, ((q % 2) * 2 + q // 8 - z) % 4
    rv, ru = jnp.where(core == 0, rz, ry), jnp.where(core == 0, ry, rz)
    place = (rv * 4 + ru).astype(jnp.int32)

    factor = jnp.exp2(weight_scales.astype(F32))
    wrows, wcols = weight_codes.shape
    weight = weight_codes.astype(F32).reshape(2, wrows // 2, wcols) * factor[:, None, :]
    weight = weight.reshape(wrows, wcols).astype(BF16)
    hc = wcols // 2
    keep = jnp.where(core == 0, weight[:, :hc], weight[:, hc:])
    send = jnp.where(core == 0, weight[:, hc:], weight[:, :hc])
    got = permute(send, SWAP)
    chip = jnp.where(
        core == 0, jnp.concatenate([keep, got], 0), jnp.concatenate([got, keep], 0)
    )
    tokens_later, chip = lax.optimization_barrier((tokens, chip))
    tokens_sib = permute(tokens_later, SWAP)
    ring = collect(chip, along_x)
    ordered = []
    for i in range(4):
        r = (i - x) % 4
        ordered.append(
            jnp.where(r == 0, ring[0], jnp.where(r == 1, ring[1], jnp.where(r == 2, ring[2], ring[3])))
        )
    block = jnp.concatenate(ordered, 0)
    plane = jnp.stack(collect(block, along_u))
    plane, tokens_now, tokens_sib, order, place = lax.optimization_barrier(
        (plane, tokens, tokens_sib, order, place)
    )
    w_own = [plane] + [permute(plane, along_v(d)) for d in (-1, 2, 1)]

    acc = keys_part(order, tokens, tokens_sib, w_own[:1], None, (0,))
    inv, bias = prepare(tokens_now, doc_ids)
    w_own[2], inv, bias, *acc = lax.optimization_barrier((w_own[2], inv, bias, *acc))
    acc = keys_part(order, tokens, tokens_sib, w_own[2:3], acc, (2,))
    w_own[3], w_own[1], *acc = lax.optimization_barrier((w_own[3], w_own[1], *acc))
    keys_own, keys_sib = keys_part(order, tokens, tokens_sib, w_own[1::2], acc, (1, 3))
    keys_oth = permute(keys_sib, SWAP)
    w_sib = [permute(w, SWAP) for w in w_own]

    out, dk, dkw_own, dkw_oth, ms = attention(
        queries, keys_own, keys_oth, values, out_grad, inv, bias
    )
    dkw_oth, *w_sib = lax.optimization_barrier((dkw_oth, *w_sib))
    dkw_sib = permute(dkw_oth, SWAP)

    parts = [None] * 4
    for r in (2, 1, 3, 0):
        parts[r] = grad_part(order, tokens, tokens_sib, dkw_own, dkw_sib, r)
    arrived = distribute(parts, along_v)
    grad_tokens = token_grad(place, tokens, dk, w_own, w_sib, inv, ms)
    two, right, left = arrived
    grad_tokens, own, two = lax.optimization_barrier((grad_tokens, parts[0], two))
    early = own.astype(F32) + two.astype(F32)
    early, right, left = lax.optimization_barrier((early, right, left))

    def total(own, others):
        s = own.astype(F32)
        for o in others:
            s = s + o.astype(F32)
        return s

    chunk = [total(early[r], [right[r], left[r]]) for r in range(4)]
    arrived = distribute([c.astype(BF16) for c in chunk], along_u)
    line = total(chunk[0], arrived)
    by_x = [lax.dynamic_slice_in_dim(line, ((x + r) % 4) * HD, HD, 1) for r in range(4)]
    arrived = distribute([c.astype(BF16) for c in by_x], along_x)
    mine = total(by_x[0], arrived).T
    keep = lax.dynamic_slice_in_dim(mine, core * wrows, wrows, 0)
    got = permute(lax.dynamic_slice_in_dim(mine, (1 - core) * wrows, wrows, 0), SWAP)
    grad_weight = jnp.where(
        core == 0, jnp.concatenate([keep, got], 1), jnp.concatenate([got, keep], 1)
    )
    return (out, grad_tokens, grad_weight)


def solution(mesh):
    return jax.shard_map(
        per_device,
        mesh=mesh,
        in_specs=(
            P(("outer", "inner"), None),
            P(("outer", "inner"), None),
            P(("outer", "inner"), None),
            P(("outer", "inner"), None),
            P(("inner", "outer"), None),
            P(("inner", "outer"), None),
            P(("outer", "inner"), None),
        ),
        out_specs=(
            P(("outer", "inner"), None),
            P(("outer", "inner"), None),
            P(("inner", "outer"), None),
        ),
        check_vma=False,
    )
```
